256 devices in a mesh: lon: 32 (over x_lo, z, core), lat: 8 (over y, x_hi).
Axes of the slice: x: 4 (x_hi: 2, x_lo: 2; x = x_hi * 2 + x_lo), y: 4, z: 8, core: 2. Of those that a mesh axis runs over, the one named last changes fastest.
Arguments:
- thermal_anomaly_field: float32 [15, 768, 4096], P(None, 'lat', 'lon'), may hold values from -6 to 6
- saltiness_anomaly: float32 [15, 768, 4096], P(None, 'lat', 'lon'), may hold values from -6 to 6
- zonal_boundary_flow: float32 [15, 768, 4096], P(None, 'lat', 'lon'), may hold values from -3 to 3
- meridional_boundary_flow: float32 [15, 768, 4096], P(None, 'lat', 'lon'), may hold values from -3 to 3
- navigable_water_flag: int32 [15, 768, 4096], P(None, 'lat', 'lon'), may hold values 0 or 1
- flooded_layer_tally: int32 [768, 4096], P('lat', 'lon'), may hold values from 0 to 15, as said below
Outputs:
- temperature_next: float32 [15, 768, 4096], P(None, 'lat', 'lon')
- salinity_next: float32 [15, 768, 4096], P(None, 'lat', 'lon')
- zonal_next: float32 [15, 768, 4096], P(None, 'lat', 'lon')
- meridional_next: float32 [15, 768, 4096], P(None, 'lat', 'lon')
The draws below stay inside these ranges and needn't reach their ends.
Inputs may be any that keep to these rules, and one draw needn't show every extreme that they name: `flooded_layer_tally`: land columns have 0.
All inputs are finite; a program needn't handle non-finite values. No bound on the sum of `navigable_water_flag` on one device may be relied on, other than what follows from the above.
Results may differ from the reference program's by a relative error of at most 0.0003.
Values sent between devices are 32-bit elements; how exact they have to be, the bound alone decides.
No kernel may reach another device: no remote copies, remote signals or barrier semaphores. Data moves between devices by JAX's collectives and lax.ppermute only.
A program may use at most 64 MiB of HBM per device.

```python
import jax
import jax.numpy as jnp

VERT_LAYERS = 15
CJ = 96
CI = 128
STEPS = 2
MERIDIAN_ROWS = 768
ZONAL_STRIPS = 4096


def draw_flooded_layer_tally(key, part):
    key = jax.random.fold_in(key, 7)
    first_key, second_key, third_key = jax.random.split(key, 3)
    depths = jax.random.randint(first_key, (MERIDIAN_ROWS, ZONAL_STRIPS), 1, VERT_LAYERS + 1)
    block_rows = MERIDIAN_ROWS // CJ
    block_cols = ZONAL_STRIPS // CI
    block_land = jax.random.randint(second_key, (block_rows, block_cols), 0, 4) == 0
    block_land = block_land.at[0, 0].set(True)
    cell_land = jax.random.randint(third_key, (MERIDIAN_ROWS, ZONAL_STRIPS), 0, 6) == 0
    land = jnp.repeat(jnp.repeat(block_land, CJ, axis=0), CI, axis=1) | cell_land
    return jnp.where(land, 0, depths).astype(jnp.int32)


def set_ends(drawn, key, smallest, largest):
    spot = [jax.random.randint(jax.random.fold_in(key, axis), (), 0, length) for axis, length in enumerate(drawn.shape)]
    widest = drawn.shape.index(max(drawn.shape))
    next_to = spot[:widest] + [(spot[widest] + 1) % drawn.shape[widest]] + spot[widest + 1:]
    return drawn.at[tuple(spot)].set(smallest).at[tuple(next_to)].set(largest)


def levels(own_key, dims, cuts, least, largest):
    loudness = 1.0
    for dim, shards_of in cuts:
        steps = jax.random.uniform(jax.random.fold_in(jax.random.fold_in(own_key, 6), dim), (shards_of,), jnp.float32, least / len(cuts), largest / len(cuts))
        loudness = loudness * jnp.repeat(jnp.exp(steps), dims[dim] // shards_of).reshape((-1,) + (1,) * (len(dims) - 1 - dim))
    return loudness


def gaussian(key, shape, width, most, shards=(), kind=jnp.bfloat16):
    factor_of = levels(key, shape, shards, -0.22, 0.18) if shards else 1.0
    values = jax.random.normal(key, shape, jnp.float32) * width * factor_of
    return jnp.minimum(jnp.maximum(values, -most), most).astype(kind)


def setup_inputs(seed: int = 0) -> dict:
    streams_of = jax.random.split(jax.random.key(seed), 7)
    return {
        "thermal_anomaly_field": gaussian(streams_of[0], (VERT_LAYERS, MERIDIAN_ROWS, ZONAL_STRIPS), 1.0, 6.0, ((1, 8), (2, 32)), jnp.float32),
        "saltiness_anomaly": gaussian(streams_of[1], (VERT_LAYERS, MERIDIAN_ROWS, ZONAL_STRIPS), 1.0, 6.0, ((1, 8), (2, 32)), jnp.float32),
        "zonal_boundary_flow": gaussian(streams_of[2], (VERT_LAYERS, MERIDIAN_ROWS, ZONAL_STRIPS), 0.5, 3.0, ((1, 8), (2, 32)), jnp.float32),
        "meridional_boundary_flow": gaussian(streams_of[3], (VERT_LAYERS, MERIDIAN_ROWS, ZONAL_STRIPS), 0.5, 3.0, ((1, 8), (2, 32)), jnp.float32),
        "navigable_water_flag": set_ends((jax.random.randint(streams_of[4], (VERT_LAYERS, MERIDIAN_ROWS, ZONAL_STRIPS), 0, 10) < 9).astype(jnp.int32), jax.random.fold_in(streams_of[4], 1), 0, 1),
        "flooded_layer_tally": draw_flooded_layer_tally(jax.random.fold_in(streams_of[6], 71), 0),
    }


TIME_STEP = 0.2
KAPPA = 0.1
VISCOSITY = 0.1
VERTICAL = 0.5
GRAVITY = 0.2
THERMAL = 0.3
HALINE = 0.2
CORIOLIS = 0.5


def shifted(field, row_off, col_off):
    row_count = field.shape[-2] - 2
    col_count = field.shape[-1] - 2
    return field[..., 1 + row_off:1 + row_off + row_count, 1 + col_off:1 + col_off + col_count]


def upwind(speed, donor_low, donor_high):
    return speed * jnp.where(speed > 0, donor_low, donor_high)


def laplace(field_ext):
    return (shifted(field_ext, 0, 1) + shifted(field_ext, 0, -1) + shifted(field_ext, 1, 0)
            + shifted(field_ext, -1, 0) - 4.0 * shifted(field_ext, 0, 0))


def vertical_mixing(tracers, wet_here):
    level_count = wet_here.shape[0]
    links = [VERTICAL * wet_here[level] * wet_here[level + 1] for level in range(level_count - 1)]
    zero_link = jnp.zeros_like(wet_here[0])
    pivots = []
    partial_values = []
    for level in range(level_count):
        upper = links[level - 1] if level > 0 else zero_link
        lower = links[level] if level < level_count - 1 else zero_link
        diagonal = 1.0 + upper + lower
        if level == 0:
            pivot = diagonal
            value = tracers[:, 0] / pivot
        else:
            pivot = diagonal - upper * upper / pivots[-1]
            value = (tracers[:, level] + upper * partial_values[-1]) / pivot
        pivots.append(pivot)
        partial_values.append(value)
    results = [partial_values[-1]]
    for level in range(level_count - 2, -1, -1):
        results.append(partial_values[level] + links[level] * results[-1] / pivots[level])
    return jnp.stack(results[::-1], axis=1)


def advance(extended, wet_ext, coriolis):
    temp_ext, salt_ext, u_ext, v_ext = extended[0], extended[1], extended[2], extended[3]
    wet_here = shifted(wet_ext, 0, 0)
    east_open = wet_here * shifted(wet_ext, 0, 1)
    west_open = wet_here * shifted(wet_ext, 0, -1)
    north_open = wet_here * shifted(wet_ext, 1, 0)
    south_open = wet_here * shifted(wet_ext, -1, 0)
    u_east = shifted(u_ext, 0, 0)
    u_west = shifted(u_ext, 0, -1)
    v_north = shifted(v_ext, 0, 0)
    v_south = shifted(v_ext, -1, 0)

    def transport(tracer_ext):
        here = shifted(tracer_ext, 0, 0)
        east = shifted(tracer_ext, 0, 1)
        west = shifted(tracer_ext, 0, -1)
        north = shifted(tracer_ext, 1, 0)
        south = shifted(tracer_ext, -1, 0)
        flux_east = east_open * upwind(u_east, here, east)
        flux_west = west_open * upwind(u_west, west, here)
        flux_north = north_open * upwind(v_north, here, north)
        flux_south = south_open * upwind(v_south, south, here)
        mixing = (east_open * (east - here) + west_open * (west - here)
                  + north_open * (north - here) + south_open * (south - here))
        return wet_here * (here - TIME_STEP * (flux_east - flux_west + flux_north - flux_south)
                           + TIME_STEP * KAPPA * mixing)

    tracers = jnp.stack([transport(temp_ext), transport(salt_ext)])
    tracers = vertical_mixing(tracers, wet_here)
    density = HALINE * salt_ext - THERMAL * temp_ext
    pressure = GRAVITY * (jnp.cumsum(density, axis=0) - 0.5 * density)
    press_here = shifted(pressure, 0, 0)
    press_east = shifted(pressure, 0, 1)
    press_north = shifted(pressure, 1, 0)
    rotation = coriolis[None, :, None]
    v_at_u = 0.25 * (shifted(v_ext, 0, 0) + shifted(v_ext, 0, 1) + shifted(v_ext, -1, 0) + shifted(v_ext, -1, 1))
    u_at_v = 0.25 * (shifted(u_ext, 0, 0) + shifted(u_ext, 0, -1) + shifted(u_ext, 1, 0) + shifted(u_ext, 1, -1))
    u_next = east_open * (u_east + TIME_STEP * (rotation * v_at_u - (press_east - press_here)
                                                + VISCOSITY * laplace(u_ext)))
    v_next = north_open * (v_north + TIME_STEP * (-rotation * u_at_v - (press_north - press_here)
                                                  + VISCOSITY * laplace(v_ext)))
    return jnp.concatenate([tracers, u_next[None], v_next[None]], axis=0)


def extend_global(fields, field_signs):
    north_row = field_signs * jnp.flip(fields[:, :, -1, :], axis=-1)
    south_row = jnp.zeros_like(north_row)
    padded = jnp.concatenate([south_row[:, :, None, :], fields, north_row[:, :, None, :]], axis=2)
    return jnp.concatenate([padded[..., -1:], padded, padded[..., :1]], axis=3)


def reference(thermal_anomaly_field, saltiness_anomaly, zonal_boundary_flow, meridional_boundary_flow, navigable_water_flag, flooded_layer_tally):
    level_count = navigable_water_flag.shape[0]
    level_index = jnp.arange(level_count, dtype=jnp.int32)[:, None, None]
    flooded_grid_indicator = (navigable_water_flag * (level_index < flooded_layer_tally[None]).astype(jnp.int32)).astype(jnp.float32)
    wet_ext = extend_global(flooded_grid_indicator[None], jnp.ones((1, 1, 1), jnp.float32))[0]
    row_index = jnp.arange(MERIDIAN_ROWS, dtype=jnp.float32)
    coriolis = CORIOLIS * jnp.sin(jnp.pi * ((row_index + 0.5) / MERIDIAN_ROWS - 0.3))
    field_signs = jnp.array([1.0, 1.0, -1.0, -1.0], jnp.float32)[:, None, None]
    marine_condition = jnp.stack([thermal_anomaly_field, saltiness_anomaly, zonal_boundary_flow, meridional_boundary_flow])
    for step_number in range(STEPS):
        marine_condition = advance(extend_global(marine_condition, field_signs), wet_ext, coriolis)
    return marine_condition[0], marine_condition[1], marine_condition[2], marine_condition[3]
```

```python
import jax
import jax.numpy as jnp
from jax import lax
from jax.experimental import pallas as pl
from jax.experimental.pallas import tpu as pltpu
from jax.sharding import PartitionSpec as P

TIME_STEP = 0.2
KAPPA = 0.1
VISCOSITY = 0.1
VERTICAL = 0.5
GRAVITY = 0.2
THERMAL = 0.3
HALINE = 0.2
CORIOLIS = 0.5

LEVELS = 15
ROWS = 96
COLS = 128
TILE = 8
BLOCKS = ROWS // TILE
PAD = TILE
TALL = ROWS + 2 * PAD
FIELDS = 5
STATE = 4
SIGNS = (1.0, 1.0, -1.0, -1.0, 1.0)
PACK = 16 * 2 * FIELDS
WET_AT = 8 * LEVELS
EDGE_AT = WET_AT + 32
MESSAGE = EDGE_AT + 16
VMEM = pltpu.CompilerParams(vmem_limit_bytes=48 * 1024 * 1024)
F32 = jnp.float32


def roll(x, shift, axis):
    return pltpu.roll(x, shift % x.shape[axis], axis)


def iota(shape, axis):
    return lax.broadcasted_iota(jnp.int32, shape, axis)


def links_of(wet):
    out = []
    above, ratio = None, None
    for k in range(LEVELS):
        below = VERTICAL * wet[k] * wet[k + 1] if k < LEVELS - 1 else None
        pivot = 1.0 + (below if below is not None else 0.0)
        if above is not None:
            pivot = pivot + above - above * ratio
        inverse = 1.0 / pivot
        ratio = below * inverse if below is not None else None
        out.append((above, inverse, ratio))
        above = below
    return out


def column_step(get, faces, links, spin):
    mix = KAPPA
    half = 0.5 * GRAVITY * TIME_STEP
    done = [[], [], [], []]
    forward = []
    east_sum = north_sum = None
    for k in range(LEVELS):
        w, oe, ow, on, os = faces(k)
        u, uE, uW, uN, uS = (get(2, k, 0, 0), get(2, k, 0, 1), get(2, k, 0, -1), get(2, k, 1, 0), get(2, k, -1, 0))
        v, vE, vW, vN, vS = (get(3, k, 0, 0), get(3, k, 0, 1), get(3, k, 0, -1), get(3, k, 1, 0), get(3, k, -1, 0))
        uNW, vSE = get(2, k, 1, -1), get(3, k, -1, 1)
        coef = []
        for speed, face in ((u, oe), (uW, ow), (v, on), (vS, os)):
            low = jnp.maximum(speed, 0.0) + mix
            coef.append((face * low, face * (low - speed)))
        tracers = []
        east, north = [], []
        for f in (0, 1):
            c, cE, cW, cN, cS = (get(f, k, 0, 0), get(f, k, 0, 1), get(f, k, 0, -1), get(f, k, 1, 0), get(f, k, -1, 0))
            out_e = coef[0][0] * c - coef[0][1] * cE
            out_w = coef[1][0] * cW - coef[1][1] * c
            out_n = coef[2][0] * c - coef[2][1] * cN
            out_s = coef[3][0] * cS - coef[3][1] * c
            tracers.append(w * (c - TIME_STEP * ((out_e - out_w) + (out_n - out_s))))
            east.append(cE - c)
            north.append(cN - c)
        up, inverse, _ = links(k)
        if k:
            before = forward[-1]
            forward.append(tuple((x + up * y) * inverse for x, y in zip(tracers, before)))
        else:
            forward.append(tuple(x * inverse for x in tracers))
        east_now = (half * HALINE) * east[1] - (half * THERMAL) * east[0]
        north_now = (half * HALINE) * north[1] - (half * THERMAL) * north[0]
        east_p = east_now if k == 0 else east_sum + east_now
        north_p = north_now if k == 0 else north_sum + north_now
        east_sum, north_sum = east_p + east_now, north_p + north_now
        turn = TIME_STEP * VISCOSITY
        done[2].append(oe * ((1.0 - 4.0 * turn) * u + spin * ((v + vS) + (vE + vSE)) - east_p
                             + turn * ((uE + uW) + (uN + uS))))
        done[3].append(on * ((1.0 - 4.0 * turn) * v - spin * ((u + uN) + (uW + uNW)) - north_p
                             + turn * ((vE + vW) + (vN + vS))))
    for f in (0, 1):
        value = forward[-1][f]
        back = [value]
        for k in range(LEVELS - 2, -1, -1):
            value = forward[k][f] + links(k)[2] * value
            back.append(value)
        done[f] = back[::-1]
    return done


def spin_of(row_index):
    angle = jnp.pi * ((row_index + 0.5) / (8.0 * ROWS) - 0.3)
    return (0.25 * TIME_STEP * CORIOLIS) * jnp.sin(angle)


def memo(shift, fields):
    held = {}

    def get(f, k, dj, di):
        key = (f, k, dj, di)
        if key not in held:
            held[key] = fields[f][k] if dj == 0 and di == 0 else shift(fields[f][k], dj, di)
        return held[key]

    return get


def faces_of(get):
    def faces(k):
        w = get(4, k, 0, 0)
        return (w, w * get(4, k, 0, 1), w * get(4, k, 0, -1), w * get(4, k, 1, 0), w * get(4, k, -1, 0))

    return faces


def pack_kernel(place, t, s, u, v, flag, tally, col_p, col_q, own_cols, rows, scratch):
    odd = place[1] % 2 == 1
    lane = iota((ROWS, COLS), 1)
    deep = tally[...]
    for f in range(FIELDS):
        gathered = jnp.zeros((ROWS, COLS), F32)
        for k in range(LEVELS):
            if f < STATE:
                x = (t, s, u, v)[f][k]
            else:
                x = jnp.where(k < deep, flag[k], 0).astype(F32)
            gathered = jnp.where((lane >= 8 * k) & (lane < 8 * k + 4), roll(x, 8 * k + 2, 1), gathered)
            at = 8 * k + 2 * f if f < STATE else WET_AT + 2 * k
            rows[0, at:at + 2, :] = x[0:2]
            rows[1, at:at + 2, :] = x[ROWS - 2:ROWS]
        scratch[0:ROWS, :] = gathered
        scratch[ROWS:COLS, :] = jnp.zeros((COLS - ROWS, COLS), F32)
        own_cols[f] = scratch[...].T
        for c in range(2):
            last = own_cols[f, pl.ds(c, 16, stride=8), :]
            first = own_cols[f, pl.ds(2 + c, 16, stride=8), :]
            at = (2 * f + c) * 16
            col_p[at:at + 16, :] = jnp.where(odd, first, last)
            col_q[at:at + 16, :] = jnp.where(odd, last, first)
    rows[0, WET_AT + 30:EDGE_AT, :] = jnp.zeros((2, COLS), F32)
    rows[1, WET_AT + 30:EDGE_AT, :] = jnp.zeros((2, COLS), F32)


def spread_kernel(place, got_p, got_q, own_cols, rows, strip, ghost, own, to_x, to_y, turned):
    odd = place[1] % 2 == 1
    lat_odd = place[0] % 2 == 1
    fold = place[0] == 7
    for f in range(FIELDS):
        for c in range(2):
            at = (2 * f + c) * 16
            a, b = got_p[at:at + 16, :], got_q[at:at + 16, :]
            west, east = jnp.where(odd, a, b), jnp.where(odd, b, a)
            strip[f, pl.ds(c, 16, stride=8), :] = west
            strip[f, pl.ds(4 + c, 16, stride=8), :] = east
            turned[pl.ds(c, 16, stride=8), :] = west
            turned[pl.ds(2 + c, 16, stride=8), :] = east
            turned[pl.ds(4 + c, 16, stride=8), :] = west
            turned[pl.ds(6 + c, 16, stride=8), :] = east
        strip[f, pl.ds(2, 16, stride=8), :] = own_cols[f, pl.ds(2, 16, stride=8), :]
        strip[f, pl.ds(3, 16, stride=8), :] = own_cols[f, pl.ds(1, 16, stride=8), :]
        strip[f, pl.ds(6, 16, stride=8), :] = jnp.zeros((16, COLS), F32)
        strip[f, pl.ds(7, 16, stride=8), :] = jnp.zeros((16, COLS), F32)
        ghost[f] = turned[...].T
        own[0, EDGE_AT + 2 * f:EDGE_AT + 2 * f + 2, :] = ghost[f, 0:2, :]
        own[1, EDGE_AT + 2 * f:EDGE_AT + 2 * f + 2, :] = ghost[f, ROWS - 2:ROWS, :]
    for side in range(2):
        own[side, 0:EDGE_AT, :] = rows[side]
        own[side, EDGE_AT + 2 * FIELDS:MESSAGE, :] = jnp.zeros((MESSAGE - EDGE_AT - 2 * FIELDS, COLS), F32)
    low, high = own[0], own[1]
    to_x[...] = jnp.where(lat_odd, high, low)
    to_y[...] = jnp.where(lat_odd, low, high)

    @pl.when(fold)
    def _():
        a, b = iota((COLS, COLS), 0), iota((COLS, COLS), 1)
        mirror = (a + b == COLS - 1).astype(F32)
        mirror_edge = ((a // 8 == b // 8) & (a % 8 < 4) & (a % 8 + b % 8 == 3)).astype(F32)
        to_x[0:EDGE_AT, :] = jnp.dot(own[1, 0:EDGE_AT, :], mirror, precision=lax.Precision.HIGHEST,
                                     preferred_element_type=F32)
        to_x[EDGE_AT:MESSAGE, :] = jnp.dot(own[1, EDGE_AT:MESSAGE, :], mirror_edge,
                                           precision=lax.Precision.HIGHEST, preferred_element_type=F32)


def inner_kernel(place, t, s, u, v, flag, tally, strip, ghost, t_out, s_out, u_out, v_out, inner, inner_ghost,
                 field, east, west, wet, oe, ow, on, link, ghost1, turned):
    first_row = place[0] * ROWS
    lane = iota((TILE, COLS), 1)
    sub = iota((TILE, COLS), 0)

    def at(b):
        return pl.multiple_of(b * TILE + PAD, TILE)

    def sides(x, edge, k):
        h = roll(edge, 126 - 8 * k, 1)
        return (roll(jnp.where(lane == 0, h, x), COLS - 1, 1), roll(jnp.where(lane == COLS - 1, h, x), 1, 1))

    def wet_block(b, carry):
        r = at(b)
        src = pl.ds(pl.multiple_of(b * TILE, TILE), TILE)
        deep = tally[src, :]
        edge = ghost[4, src, :]
        column = []
        for k in range(LEVELS):
            w = jnp.where(k < deep, flag[k, src, :], 0).astype(F32)
            column.append(w)
            wet[k, pl.ds(r, TILE), :] = w
            e, a = sides(w, edge, k)
            oe[k, pl.ds(r, TILE), :] = w * e
            ow[k, pl.ds(r, TILE), :] = w * a
        for k, (up, inverse, ratio) in enumerate(links_of(column)):
            if up is not None:
                link[0, k, src, :] = up
            link[1, k, src, :] = inverse
            if ratio is not None:
                link[2, k, src, :] = ratio
        return carry

    lax.fori_loop(0, BLOCKS, wet_block, 0)

    def north_block(b, carry):
        r = at(b)
        for k in range(LEVELS):
            on[k, pl.ds(r, TILE), :] = wet[k, pl.ds(r, TILE), :] * wet[k, pl.ds(r + 1, TILE), :]
        return carry

    lax.fori_loop(0, BLOCKS, north_block, 0)

    def strip_shift(x, dj, di):
        if di:
            x = roll(x, -di, 0)
        return roll(x, -dj, 1) if dj else x

    values = [[strip[f, 8 * k:8 * k + 8, :] for k in range(LEVELS)] for f in range(FIELDS)]
    get = memo(strip_shift, values)
    row = (first_row + iota((1, COLS), 1)).astype(F32)
    links = links_of(values[4])
    moved = column_step(get, faces_of(get), lambda k: links[k], spin_of(row))
    for f in range(STATE):
        for k in range(LEVELS):
            turned[8 * k:8 * k + 8, :] = jnp.where(sub == 1, moved[f][k], roll(moved[f][k], -2, 0))
        turned[8 * LEVELS:COLS, :] = jnp.zeros((COLS - 8 * LEVELS, COLS), F32)
        ghost1[f] = turned[...].T

    for step in range(2):
        def spread_block(b, carry, step=step):
            r = at(b)
            src = pl.ds(pl.multiple_of(b * TILE, TILE), TILE)
            for f in range(STATE):
                edge = (ghost, ghost1)[step][f, src, :]
                for k in range(LEVELS):
                    if step == 0:
                        x = (t, s, u, v)[f][k, src, :]
                        field[0, f, k, pl.ds(r, TILE), :] = x
                    else:
                        x = field[1, f, k, pl.ds(r, TILE), :]
                    e, a = sides(x, edge, k)
                    east[f, k, pl.ds(r, TILE), :] = e
                    west[f, k, pl.ds(r, TILE), :] = a
            return carry

        lax.fori_loop(0, BLOCKS, spread_block, 0)

        def step_block(b, carry, step=step):
            r = at(b)
            src = pl.ds(pl.multiple_of(b * TILE, TILE), TILE)

            def get(f, k, dj, di):
                ref = (field.at[step], east, west)[di]
                return ref[f, k, pl.ds(r + dj, TILE), :]

            def faces(k):
                here = pl.ds(r, TILE)
                return (wet[k, here, :], oe[k, here, :], ow[k, here, :], on[k, here, :], on[k, pl.ds(r - 1, TILE), :])

            def links(k):
                return tuple(link[i, k, src, :] for i in range(3))

            row = (first_row + b * TILE + iota((TILE, COLS), 0)).astype(F32)
            moved = column_step(get, faces, links, spin_of(row))
            for f in range(STATE):
                for k in range(LEVELS):
                    if step == 0:
                        field[1, f, k, pl.ds(r, TILE), :] = moved[f][k]
                    else:
                        (t_out, s_out, u_out, v_out)[f][k, src, :] = moved[f][k]
            return carry

        lax.fori_loop(0, BLOCKS, step_block, 0)

    for f in range(FIELDS):
        for k in range(LEVELS):
            src = field.at[1, f, k] if f < STATE else wet.at[k]
            inner[0, f, k] = src[PAD - 1:PAD + 7, :]
            inner[1, f, k] = src[PAD + 93:PAD + 101, :]
        edge = ghost1[f] if f < STATE else ghost[4]
        inner_ghost[0, f] = roll(edge[0:8], 1, 0)
        inner_ghost[1, f] = edge[93:101]


def edge_kernel(folds, place, own, got, inner, inner_ghost, t, s, u, v, t_out, s_out, u_out, v_out, lower, upper):
    lat = place[0]
    high = place[2] == 1
    fold = (lat == 7) & high if folds else None
    mine, theirs = own[0], got[...]
    if folds:
        theirs = jnp.where((lat == 0) & jnp.logical_not(high), 0.0, theirs)
    lower[...] = jnp.where(high, mine, theirs)
    upper[...] = jnp.where(high, theirs, mine)
    sub = iota((TILE, COLS), 0)
    lane = iota((TILE, COLS), 1)

    def stack(at, sign):
        a, b = lower[at:at + 2, :], upper[at:at + 2, :]
        if not folds:
            return jnp.concatenate([a, b, a, b], axis=0)
        second = jnp.where(fold, sign * b[1:2], b[0:1])
        return jnp.concatenate([a, second, b[1:2], b, sign * a[1:2], a[1:2]], axis=0)

    def spread(edge, k):
        return roll(edge, 126 - 8 * k, 1)

    values = []
    for f in range(FIELDS):
        edge = stack(EDGE_AT + 2 * f, SIGNS[f])
        levels = []
        for k in range(LEVELS):
            x = stack(8 * k + 2 * f if f < STATE else WET_AT + 2 * k, SIGNS[f])
            levels.append(jnp.concatenate([x, spread(edge, k)], axis=1))
        values.append(levels)

    back = iota((TILE, 2 * COLS), 0) >= jnp.where(fold, 4, TILE) if folds else None

    def ring_shift(x, dj, di):
        if dj:
            x = roll(x, -dj, 0)
        if di:
            there = roll(x, -di, 1)
            x = jnp.where(back, roll(x, di, 1), there) if folds else there
        return x

    def rows_of(start, shape):
        return (lat * ROWS + start + iota(shape, 0)).astype(F32)

    get = memo(ring_shift, values)
    links = links_of(values[4])
    start = jnp.where(high, ROWS - 2, -2)
    row = rows_of(start, (TILE, 1))
    if folds:
        row = jnp.where(fold, float(8 * ROWS - 1), row)
    moved = column_step(get, faces_of(get), lambda k: links[k], spin_of(row))

    def settle(x, f):
        ring = x
        up = roll(ring, 1, 0)
        down = roll(ring, -1, 0)
        if folds:
            up = jnp.where(sub == jnp.where(fold, 3, TILE), SIGNS[f] * roll(ring, -2, 0), up)
        return jnp.where(high, up, down)

    fresh_at = jnp.where(high, 2, 0)
    fresh = (sub >= fresh_at) & (sub < fresh_at + 2)
    middles, ghosts = [], []
    for f in range(FIELDS):
        mids, eds = [], []
        near = inner_ghost[0, f]
        for k in range(LEVELS):
            part = moved[f][k] if f < STATE else values[4][k]
            mids.append(jnp.where(fresh, settle(part[:, :COLS], f), inner[0, f, k]))
            eds.append(jnp.where(fresh, settle(part[:, COLS:], f), spread(near, k)))
        middles.append(mids)
        ghosts.append(eds)
    held = {}

    def get2(f, k, dj, di):
        key = (f, k, dj, di)
        if key not in held:
            x = middles[f][k]
            if di == 1:
                x = roll(jnp.where(lane == 0, ghosts[f][k], x), COLS - 1, 1)
            elif di == -1:
                x = roll(jnp.where(lane == COLS - 1, ghosts[f][k], x), 1, 1)
            held[key] = roll(x, -dj, 0) if dj else x
        return held[key]

    links2 = links_of(middles[4])
    row2 = rows_of(jnp.where(high, ROWS - 3, -1), (TILE, 1))
    last = column_step(get2, faces_of(get2), lambda k: links2[k], spin_of(row2))
    write_at = jnp.where(high, TILE - 2, 0)
    write = (sub >= write_at) & (sub < write_at + 2)
    for f in range(STATE):
        for k in range(LEVELS):
            x = jnp.where(high, roll(last[f][k], 5, 0), roll(last[f][k], -1, 0))
            (t_out, s_out, u_out, v_out)[f][k] = jnp.where(write, x, (t, s, u, v)[f][k])


def whole(shape):
    return pl.BlockSpec(shape, lambda *_: (0,) * len(shape))


def call(kernel, place, args, outs, scratch, cost):
    return pl.pallas_call(
        kernel,
        out_shape=[jax.ShapeDtypeStruct(o, F32) for o in outs],
        grid_spec=pltpu.PrefetchScalarGridSpec(
            num_scalar_prefetch=1,
            grid=(1,),
            in_specs=[whole(a.shape) for a in args],
            out_specs=[whole(o) for o in outs],
            scratch_shapes=[pltpu.VMEM(x, F32) for x in scratch],
        ),
        compiler_params=VMEM,
        cost_estimate=cost,
    )(place, *args)


def edge_call(folds, place, own, got, inner, inner_ghost, fields):
    def block(shape, index):
        return pl.BlockSpec(shape, index)

    strip = pl.BlockSpec((LEVELS, TILE, COLS), lambda i, p: (0, p[2] * (BLOCKS - 1), 0))
    return pl.pallas_call(
        lambda *refs: edge_kernel(folds, *refs),
        out_shape=[jax.ShapeDtypeStruct(x.shape, F32) for x in fields],
        grid_spec=pltpu.PrefetchScalarGridSpec(
            num_scalar_prefetch=1,
            grid=(1,),
            in_specs=[
                block((1, MESSAGE, COLS), lambda i, p: (p[2], 0, 0)),
                whole((MESSAGE, COLS)),
                block((1, FIELDS, LEVELS, TILE, COLS), lambda i, p: (p[2], 0, 0, 0, 0)),
                block((1, FIELDS, TILE, COLS), lambda i, p: (p[2], 0, 0, 0)),
            ] + [strip] * STATE,
            out_specs=[strip] * STATE,
            scratch_shapes=[pltpu.VMEM((MESSAGE, COLS), F32)] * 2,
        ),
        input_output_aliases={5 + f: f for f in range(STATE)},
        compiler_params=VMEM,
        cost_estimate=pl.CostEstimate(flops=2_000_000, bytes_accessed=2_000_000, transcendentals=0),
    )(place, own, got, inner, inner_ghost, *fields)


def device(lon, lat, lats, lons):
    return lon % lons * lats + lat


def body(t, s, u, v, flag, tally):
    lons, lats = lax.axis_size("lon"), lax.axis_size("lat")
    lat, lon = lax.axis_index("lat"), lax.axis_index("lon")
    side_x = lat % 2
    place = jnp.stack([lat, lon, side_x]).astype(jnp.int32)
    place_y = jnp.stack([lat, lon, 1 - side_x]).astype(jnp.int32)
    pairs_p, pairs_q, pairs_x, pairs_y = [], [], [], []
    for a in range(lats):
        for o in range(lons):
            here = device(o, a, lats, lons)
            pairs_p.append((here, device(o ^ 1, a, lats, lons)))
            pairs_q.append((here, device(o + 1 if o % 2 else o - 1, a, lats, lons)))
            pairs_y.append((here, device(o, a ^ 1, lats, lons)))
            next_lat = a + 1 if a % 2 else a - 1
            inside = 0 <= next_lat < lats
            pairs_x.append((here, device(o, next_lat, lats, lons) if inside else device(lons - 1 - o, a, lats, lons)))

    def send(x, pairs):
        return lax.ppermute(x, ("lon", "lat"), pairs)

    small = pl.CostEstimate(flops=1_000_000, bytes_accessed=4_000_000, transcendentals=0)
    large = pl.CostEstimate(flops=100_000_000, bytes_accessed=8_000_000, transcendentals=0)
    col_p, col_q, own_cols, rows = call(
        pack_kernel, place, (t, s, u, v, flag, tally),
        [(PACK, COLS), (PACK, COLS), (FIELDS, COLS, COLS), (2, EDGE_AT, COLS)],
        [(COLS, COLS)], small)
    got_p, got_q = send(col_p, pairs_p), send(col_q, pairs_q)
    strip, ghost, own, to_x, to_y = call(
        spread_kernel, place, (got_p, got_q, own_cols, rows),
        [(FIELDS, COLS, COLS), (FIELDS, COLS, COLS), (2, MESSAGE, COLS), (MESSAGE, COLS), (MESSAGE, COLS)],
        [(COLS, COLS)], small)
    got_x, got_y = send(to_x, pairs_x), send(to_y, pairs_y)
    tall = (LEVELS, TALL, COLS)
    *fields, inner, inner_ghost = call(
        inner_kernel, place, (t, s, u, v, flag, tally, strip, ghost),
        [(LEVELS, ROWS, COLS)] * STATE + [(2, FIELDS, LEVELS, TILE, COLS), (2, FIELDS, TILE, COLS)],
        [(2, STATE) + tall, (STATE,) + tall, (STATE,) + tall, tall, tall, tall, tall,
         (3, LEVELS, ROWS, COLS), (STATE, COLS, COLS), (COLS, COLS)], large)
    fields = edge_call(False, place_y, own, got_y, inner, inner_ghost, fields)
    fields = edge_call(True, place, own, got_x, inner, inner_ghost, fields)
    return tuple(fields)


def solution(mesh):
    cut = P(None, "lat", "lon")
    return jax.shard_map(
        body,
        mesh=mesh,
        in_specs=(cut, cut, cut, cut, cut, P("lat", "lon")),
        out_specs=(cut, cut, cut, cut),
        check_vma=False,
    )
```

```python
import jax
import jax.numpy as jnp
from jax import lax
from jax.experimental import pallas as pl
from jax.experimental.pallas import tpu as pltpu
from jax.sharding import PartitionSpec as P

TIME_STEP = 0.2
KAPPA = 0.1
VISCOSITY = 0.1
VERTICAL = 0.5
GRAVITY = 0.2
THERMAL = 0.3
HALINE = 0.2
CORIOLIS = 0.5

LEVELS = 15
ROWS = 96
COLS = 128
TILE = 8
BLOCKS = ROWS // TILE
PAD = TILE
TALL = ROWS + 2 * PAD
FIELDS = 5
STATE = 4
SIGNS = (1.0, 1.0, -1.0, -1.0, 1.0)
PACK = 16 * 2 * FIELDS
WET_AT = 8 * LEVELS
EDGE_AT = WET_AT + 32
MESSAGE = EDGE_AT + 16
F32 = jnp.float32


def roll(x, shift, axis):
    return pltpu.roll(x, shift % x.shape[axis], axis)


def iota(shape, axis):
    return lax.broadcasted_iota(jnp.int32, shape, axis)


def links_of(wet):
    out = []
    above, ratio = None, None
    for k in range(LEVELS):
        below = VERTICAL * wet[k] * wet[k + 1] if k < LEVELS - 1 else None
        pivot = 1.0 + (below if below is not None else 0.0)
        if above is not None:
            pivot = pivot + above - above * ratio
        inverse = 1.0 / pivot
        ratio = below * inverse if below is not None else None
        out.append((above, inverse, ratio))
        above = below
    return out


def column_step(get, faces, links, spin, west=None, south=None):
    mix = KAPPA
    half = 0.5 * GRAVITY * TIME_STEP
    done = [[], [], [], []]
    forward, loose = [], []
    east_sum = north_sum = None
    for k in range(LEVELS):
        w, oe, ow, on, os = faces(k)
        u, uE, uW, uN, uS = (get(2, k, 0, 0), get(2, k, 0, 1), get(2, k, 0, -1), get(2, k, 1, 0), get(2, k, -1, 0))
        v, vE, vW, vN, vS = (get(3, k, 0, 0), get(3, k, 0, 1), get(3, k, 0, -1), get(3, k, 1, 0), get(3, k, -1, 0))
        uNW, vSE = get(2, k, 1, -1), get(3, k, -1, 1)
        coef = []
        for speed, face in ((u, oe), (uW, ow), (v, on), (vS, os)):
            if face is None:
                coef.append(None)
                continue
            low = jnp.maximum(speed, 0.0) + mix
            coef.append((face * low, face * (low - speed)))
        tracers = []
        east, north = [], []
        for f in (0, 1):
            c, cE, cN = get(f, k, 0, 0), get(f, k, 0, 1), get(f, k, 1, 0)
            out_e = coef[0][0] * c - coef[0][1] * cE
            if west is None:
                out_e = out_e - (coef[1][0] * get(f, k, 0, -1) - coef[1][1] * c)
            out_n = coef[2][0] * c - coef[2][1] * cN
            out_s = south(f, k, out_n) if south else coef[3][0] * get(f, k, -1, 0) - coef[3][1] * c
            tracers.append((c - TIME_STEP * (out_n - out_s), out_e))
            east.append(cE - c)
            north.append(cN - c)
        loose.append(tracers)
        east_now = (half * HALINE) * east[1] - (half * THERMAL) * east[0]
        north_now = (half * HALINE) * north[1] - (half * THERMAL) * north[0]
        east_p = east_now if k == 0 else east_sum + east_now
        north_p = north_now if k == 0 else north_sum + north_now
        east_sum, north_sum = east_p + east_now, north_p + north_now
        turn = TIME_STEP * VISCOSITY
        done[2].append(oe * ((1.0 - 4.0 * turn) * u + spin * ((v + vS) + (vE + vSE)) - east_p
                             + turn * ((uE + uW) + (uN + uS))))
        done[3].append(on * ((1.0 - 4.0 * turn) * v - spin * ((u + uN) + (uW + uNW)) - north_p
                             + turn * ((vE + vW) + (vN + vS))))
    for k in range(LEVELS):
        w = faces(k)[0]
        up, inverse, _ = links(k)
        now = []
        for f in (0, 1):
            kept, out = loose[k][f]
            x = w * (kept - TIME_STEP * (out - west(f, k, out) if west else out))
            now.append((x + up * forward[-1][f]) * inverse if k else x * inverse)
        forward.append(now)
    for f in (0, 1):
        value = forward[-1][f]
        back = [value]
        for k in range(LEVELS - 2, -1, -1):
            value = forward[k][f] + links(k)[2] * value
            back.append(value)
        done[f] = back[::-1]
    return done


def spin_of(row_index):
    angle = jnp.pi * ((row_index + 0.5) / (8.0 * ROWS) - 0.3)
    return (0.25 * TIME_STEP * CORIOLIS) * jnp.sin(angle)


SHIFTS = {0: (), 1: (), 2: (1, -1), 3: (-1, 1), 4: ()}


def eager(shift, fields):
    held = {}
    count = len(fields)
    for f in range(count):
        for k in range(LEVELS):
            held[f, k, 0, 0] = fields[f][k]
    for dj, di in ((0, 1), (0, -1), (1, 0), (-1, 0)):
        for f in range(count):
            for k in range(LEVELS):
                held[f, k, dj, di] = shift(fields[f][k], dj, di)
    for f in (2, 3):
        dj, di = SHIFTS[f]
        for k in range(LEVELS):
            held[f, k, dj, di] = shift(held[f, k, 0, di], dj, 0)
    return lambda f, k, dj, di: held[f, k, dj, di]


def faces_of(get):
    def faces(k):
        w = get(4, k, 0, 0)
        return (w, w * get(4, k, 0, 1), w * get(4, k, 0, -1), w * get(4, k, 1, 0), w * get(4, k, -1, 0))

    return faces


def split3(x):
    a = x.astype(jnp.bfloat16)
    rest = x - a.astype(F32)
    b = rest.astype(jnp.bfloat16)
    return a, b, (rest - b.astype(F32)).astype(jnp.bfloat16)


def picker(k, moves):
    source, target = iota((COLS, COLS), 0) - 8 * k, iota((COLS, COLS), 1)
    hit = jnp.zeros((COLS, COLS), jnp.bool_)
    for lane, p in moves.items():
        hit = hit | ((target == lane) & (source == p))
    return hit.astype(jnp.bfloat16)


def picked(terms, pick):
    return sum(jnp.dot(x, pick, preferred_element_type=F32) for x in terms)


AROUND = {126: 0, 127: 1, 0: 2, 1: 3}
NEXT1 = {127: 1, 0: 6}
OWN1 = {0: 2, 127: 5}
FLUX1 = {0: 1}
FACE = {0: 1, 127: 2}


def pack_kernel(place, t, s, u, v, flag, tally, col_p, col_q, own_cols, rows, wet, field, held_flag, held_tally, sems,
                gathered):
    odd = place[1] % 2 == 1
    lane = iota((TILE, COLS), 1)
    sub = iota((TILE, COLS), 0)
    group = jnp.where(lane % 8 < 4, lane // 8, -1)
    inside = pl.ds(PAD, ROWS)
    copies = [pltpu.make_async_copy(x, field.at[f, :, inside, :], sems.at[f]) for f, x in enumerate((t, s, u, v))]
    copies.append(pltpu.make_async_copy(flag, held_flag, sems.at[4]))
    copies.append(pltpu.make_async_copy(tally, held_tally, sems.at[5]))
    for f in (4, 5, 0, 1, 2, 3):
        copies[f].start()
    for f in (4, 0, 1, 2, 3):
        copies[f].wait()
        if f == STATE:
            copies[5].wait()
        for b in range(BLOCKS):
            at = PAD + TILE * b
            out = jnp.zeros((TILE, COLS), F32)
            for k in range(LEVELS):
                if f < STATE:
                    x = field[f, k, at:at + TILE, :]
                else:
                    here = slice(TILE * b, TILE * b + TILE)
                    x = jnp.where(k < held_tally[here, :], held_flag[k, here, :], 0).astype(F32)
                    wet[k, at:at + TILE, :] = x
                out = jnp.where(group == k, roll(x, 8 * k + 2, 1), out)
            gathered[f, TILE * b:TILE * b + TILE, :] = out
        gathered[f, ROWS:COLS, :] = jnp.zeros((COLS - ROWS, COLS), F32)
    for f in range(FIELDS):
        own_cols[f] = gathered[f].T
    for side, first in ((0, PAD), (1, PAD + ROWS - 2)):
        for m in range(LEVELS + 4):
            parts = []
            for i in range(4):
                at = first - 2 * i
                if m < LEVELS:
                    parts.append(field[i, m, at:at + TILE, :])
                else:
                    k = min(4 * (m - LEVELS) + i, LEVELS - 1)
                    parts.append(wet[k, at:at + TILE, :])
            rows[side, TILE * m:TILE * m + TILE, :] = jnp.where(
                sub < 2, parts[0], jnp.where(sub < 4, parts[1], jnp.where(sub < 6, parts[2], parts[3])))
    for f in range(FIELDS):
        for c in range(2):
            last = own_cols[f, pl.ds(c, 16, stride=8), :]
            first = own_cols[f, pl.ds(2 + c, 16, stride=8), :]
            at = (2 * f + c) * 16
            col_p[at:at + 16, :] = jnp.where(odd, first, last)
            col_q[at:at + 16, :] = jnp.where(odd, last, first)


def spread_kernel(place, got_p, got_q, own_cols, rows, strip, ghost, own, to_x, to_y, turned):
    odd = place[1] % 2 == 1
    lat_odd = place[0] % 2 == 1
    fold = place[0] == 7
    for f in range(FIELDS):
        for c in range(2):
            at = (2 * f + c) * 16
            a, b = got_p[at:at + 16, :], got_q[at:at + 16, :]
            west, east = jnp.where(odd, a, b), jnp.where(odd, b, a)
            strip[f, pl.ds(c, 16, stride=8), :] = west
            strip[f, pl.ds(6 + c, 16, stride=8), :] = east
            strip[f, pl.ds(2 + c, 16, stride=8), :] = own_cols[f, pl.ds(2 + c, 16, stride=8), :]
            strip[f, pl.ds(4 + c, 16, stride=8), :] = own_cols[f, pl.ds(c, 16, stride=8), :]
            turned[f, pl.ds(c, 16, stride=8), :] = west
            turned[f, pl.ds(2 + c, 16, stride=8), :] = east
            turned[f, pl.ds(4 + c, 16, stride=8), :] = west
            turned[f, pl.ds(6 + c, 16, stride=8), :] = east
    for f in range(FIELDS):
        ghost[f] = turned[f].T
    for f in range(FIELDS):
        own[0, EDGE_AT + 2 * f:EDGE_AT + 2 * f + 2, :] = ghost[f, 0:2, :]
        own[1, EDGE_AT + 2 * f:EDGE_AT + 2 * f + 2, :] = ghost[f, ROWS - 2:ROWS, :]
    for side in range(2):
        own[side, 0:EDGE_AT, :] = rows[side]
        own[side, EDGE_AT + 2 * FIELDS:MESSAGE, :] = jnp.zeros((MESSAGE - EDGE_AT - 2 * FIELDS, COLS), F32)
    low, high = own[0], own[1]
    to_x[...] = jnp.where(lat_odd, high, low)
    to_y[...] = jnp.where(lat_odd, low, high)

    @pl.when(fold)
    def _():
        a, b = iota((COLS, COLS), 0), iota((COLS, COLS), 1)
        mirror = (a + b == COLS - 1).astype(jnp.bfloat16)
        mirror_edge = ((a // 8 == b // 8) & (a % 8 < 4) & (a % 8 + b % 8 == 3)).astype(jnp.bfloat16)
        to_x[0:EDGE_AT, :] = picked(split3(own[1, 0:EDGE_AT, :]), mirror)
        to_x[EDGE_AT:MESSAGE, :] = picked(split3(own[1, EDGE_AT:MESSAGE, :]), mirror_edge)


def rows_at(b):
    return pl.multiple_of(b * TILE + PAD, TILE)


def first_kernel(place, t, s, u, v, wet, field1, open_e, link, spin, field, flux, sems):
    first_row = place[0] * ROWS
    copies = [pltpu.make_async_copy(x, field.at[f, :, pl.ds(PAD, ROWS), :], sems.at[f])
              for f, x in enumerate((t, s, u, v))]
    for c in copies:
        c.start()

    def face_block(b, carry):
        here = pl.ds(rows_at(b), TILE)
        src = pl.ds(pl.multiple_of(b * TILE, TILE), TILE)
        column = [wet[k, here, :] for k in range(LEVELS)]
        for k, w in enumerate(column):
            open_e[k, src, :] = w * roll(w, COLS - 1, 1)
        for k, (up, inverse, ratio) in enumerate(links_of(column)):
            if up is not None:
                link[0, k, src, :] = up
            link[1, k, src, :] = inverse
            if ratio is not None:
                link[2, k, src, :] = ratio
        row = (first_row + b * TILE + iota((TILE, COLS), 0)).astype(F32)
        spin[src, :] = spin_of(row)
        return carry

    lax.fori_loop(0, BLOCKS, face_block, 0)
    for c in copies:
        c.wait()

    def step_block(b, carry):
        r = rows_at(b)
        src = pl.ds(pl.multiple_of(b * TILE, TILE), TILE)

        def get(f, k, dj, di):
            x = field[f, k, pl.ds(r + dj, TILE), :]
            return roll(x, -di, 1) if di else x

        def faces(k):
            w = wet[k, pl.ds(r, TILE), :]
            return (w, open_e[k, src, :], None, w * wet[k, pl.ds(r + 1, TILE), :], None)

        def south(f, k, x):
            flux[f, k, pl.ds(r, TILE), :] = x
            return flux[f, k, pl.ds(r - 1, TILE), :]

        moved = column_step(get, faces, lambda k: tuple(link[i, k, src, :] for i in range(3)), spin[src, :],
                            lambda f, k, x: roll(x, 1, 1), south)
        for f in range(STATE):
            for k in range(LEVELS):
                field1[f, k, pl.ds(r, TILE), :] = moved[f][k]
        return carry

    lax.fori_loop(0, BLOCKS, step_block, 0)


def second_kernel(place, field1, wet, open_e, link, spin, strip, ghost, t, s, u, v, inner, inner_ghost,
                  state, outs, ghost1, turned, beside, face, flux, sems):
    first_row = place[0] * ROWS
    lane = iota((TILE, COLS), 1)

    def strip_shift(x, dj, di):
        if di:
            x = roll(x, -di, 0)
        return roll(x, -dj, 1) if dj else x

    values = [[strip[f, 8 * k:8 * k + 8, :] for k in range(LEVELS)] for f in range(FIELDS)]
    get1 = eager(strip_shift, values)
    row = (first_row + iota((1, COLS), 1)).astype(F32)
    links1 = links_of(values[4])
    moved = column_step(get1, faces_of(get1), lambda k: links1[k], spin_of(row))
    for f in range(STATE):
        for k in range(LEVELS):
            turned[f, 8 * k:8 * k + 8, :] = moved[f][k]
    faces1 = faces_of(get1)
    for f in range(2):
        for k in range(LEVELS):
            c, speed, face_e = moved[f][k], moved[2][k], faces1(k)[1]
            low = jnp.maximum(speed, 0.0) + KAPPA
            turned[STATE + f, 8 * k:8 * k + 8, :] = face_e * (low * c - (low - speed) * roll(c, -1, 0))
    for f in range(STATE + 2):
        turned[f, 8 * LEVELS:COLS, :] = jnp.zeros((COLS - 8 * LEVELS, COLS), F32)
    for f in range(STATE + 2):
        ghost1[f] = turned[f].T

    inside = pl.ds(PAD, ROWS)
    wide = iota((ROWS, COLS), 1)
    edge_lane = (wide == 0) | (wide == COLS - 1)
    face_terms = split3(ghost[4, 0:ROWS, :])
    terms = [split3(ghost1[f, 0:ROWS, :]) for f in range(STATE + 2)]
    for k in range(LEVELS):
        face[k] = picked(face_terms[:1], picker(k, FACE))
        around, own, into = picker(k, NEXT1), picker(k, OWN1), picker(k, FLUX1)
        for f in range(STATE):
            beside[f, k, inside, :] = picked(terms[f], around)
            if f < 2:
                beside[STATE + f, k, inside, :] = picked(terms[STATE + f], into)
            state[f, k, inside, :] = jnp.where(edge_lane, picked(terms[f], own), field1[f, k, inside, :])

    def copies(b):
        src = pl.ds(pl.multiple_of(b * TILE, TILE), TILE)
        return [pltpu.make_async_copy(outs.at[f, :, src, :], x.at[:, src, :], sems.at[f, b])
                for f, x in enumerate((t, s, u, v))]

    def step_block(b, carry):
        r = rows_at(b)
        src = pl.ds(pl.multiple_of(b * TILE, TILE), TILE)

        def get(f, k, dj, di):
            here = pl.ds(r + dj, TILE)
            x = state[f, k, here, :]
            if di == 0:
                return x
            return roll(jnp.where(lane == (0 if di > 0 else COLS - 1), beside[f, k, here, :], x), -di, 1)

        def faces(k):
            w = wet[k, pl.ds(r, TILE), :]
            across = w * face[k, src, :]
            return (w, jnp.where(lane == COLS - 1, across, open_e[k, src, :]), None,
                    w * wet[k, pl.ds(r + 1, TILE), :], None)

        def west(f, k, x):
            return jnp.where(lane == 0, beside[STATE + f, k, pl.ds(r, TILE), :], roll(x, 1, 1))

        def south(f, k, x):
            flux[f, k, pl.ds(r, TILE), :] = x
            return flux[f, k, pl.ds(r - 1, TILE), :]

        moved = column_step(get, faces, lambda k: tuple(link[i, k, src, :] for i in range(3)), spin[src, :], west, south)
        for f in range(STATE):
            for k in range(LEVELS):
                outs[f, k, src, :] = moved[f][k]
        for c in copies(b):
            c.start()
        return carry

    lax.fori_loop(0, BLOCKS, step_block, 0)

    for f in range(FIELDS):
        for k in range(LEVELS):
            src = state.at[f, k] if f < STATE else wet.at[k]
            inner[0, f, k] = src[PAD - 1:PAD + 7, :]
            inner[1, f, k] = src[PAD + 93:PAD + 101, :]
        edge = ghost1[f] if f < STATE else ghost[4]
        inner_ghost[0, f] = roll(edge[0:8], 1, 0)
        inner_ghost[1, f] = edge[93:101]

    def drain(b, carry):
        for c in copies(b):
            c.wait()
        return carry

    lax.fori_loop(0, BLOCKS, drain, 0)


def edge_kernel(folds, place, own, got, inner, inner_ghost, t, s, u, v, t_out, s_out, u_out, v_out, lower, upper):
    lat = place[0]
    high = place[2] == 1
    fold = (lat == 7) & high if folds else None
    mine, theirs = own[0], got[...]
    if folds:
        theirs = jnp.where((lat == 0) & jnp.logical_not(high), 0.0, theirs)
    lower[...] = jnp.where(high, mine, theirs)
    upper[...] = jnp.where(high, theirs, mine)
    sub = iota((TILE, COLS), 0)
    lane = iota((TILE, COLS), 1)

    def stack(at, sign):
        a, b = lower[at:at + 2, :], upper[at:at + 2, :]
        if not folds:
            return jnp.concatenate([a, b, a, b], axis=0)
        second = jnp.where(fold, sign * b[1:2], b[0:1])
        return jnp.concatenate([a, second, b[1:2], b, sign * a[1:2], a[1:2]], axis=0)

    edges = [stack(EDGE_AT + 2 * f, SIGNS[f]) for f in range(FIELDS)]
    edge_terms = split3(jnp.concatenate(edges, axis=0))
    near_terms = split3(jnp.concatenate([inner_ghost[0, f] for f in range(STATE)], axis=0))
    near_wet = split3(inner_ghost[0, STATE])[:1]
    spreads, nears = [[] for _ in range(FIELDS)], [[] for _ in range(FIELDS)]
    for k in range(LEVELS):
        around = picker(k, AROUND)
        found = picked(edge_terms, around)
        near = picked(near_terms, picker(k, NEXT1))
        for f in range(FIELDS):
            spreads[f].append(found[TILE * f:TILE * f + TILE])
        for f in range(STATE):
            nears[f].append(near[TILE * f:TILE * f + TILE])
        nears[STATE].append(picked(near_wet, around))
    values = [[jnp.concatenate([stack(8 * k + 2 * f if f < STATE else WET_AT + 2 * k, SIGNS[f]), spreads[f][k]], axis=1)
               for k in range(LEVELS)] for f in range(FIELDS)]

    back = iota((TILE, 2 * COLS), 0) >= jnp.where(fold, 4, TILE) if folds else None

    def ring_shift(x, dj, di):
        if dj:
            x = roll(x, -dj, 0)
        if di:
            there = roll(x, -di, 1)
            x = jnp.where(back, roll(x, di, 1), there) if folds else there
        return x

    def rows_of(start, shape):
        return (lat * ROWS + start + iota(shape, 0)).astype(F32)

    get = eager(ring_shift, values)
    links = links_of(values[4])
    start = jnp.where(high, ROWS - 2, -2)
    row = rows_of(start, (TILE, 1))
    if folds:
        row = jnp.where(fold, float(8 * ROWS - 1), row)
    moved = column_step(get, faces_of(get), lambda k: links[k], spin_of(row))

    def settle(x, f):
        ring = x
        up = roll(ring, 1, 0)
        down = roll(ring, -1, 0)
        if folds:
            up = jnp.where(sub == jnp.where(fold, 3, TILE), SIGNS[f] * roll(ring, -2, 0), up)
        return jnp.where(high, up, down)

    fresh_at = jnp.where(high, 2, 0)
    fresh = (sub >= fresh_at) & (sub < fresh_at + 2)
    middles, ghosts = [], []
    for f in range(FIELDS):
        mids, eds = [], []
        for k in range(LEVELS):
            part = moved[f][k] if f < STATE else values[4][k]
            mids.append(jnp.where(fresh, settle(part[:, :COLS], f), inner[0, f, k]))
            eds.append(jnp.where(fresh, settle(part[:, COLS:], f), nears[f][k]))
        middles.append(mids)
        ghosts.append(eds)
    for f in range(FIELDS):
        middles[f] = list(zip(middles[f], ghosts[f]))

    def shift2(pair, dj, di):
        x, ghosted = pair
        if di == 1:
            return roll(jnp.where(lane == 0, ghosted, x), COLS - 1, 1), None
        if di == -1:
            return roll(jnp.where(lane == COLS - 1, ghosted, x), 1, 1), None
        return roll(x, -dj, 0), None

    pairs = eager(shift2, middles)

    def get2(f, k, dj, di):
        return pairs(f, k, dj, di)[0]

    links2 = links_of([x for x, _ in middles[4]])
    row2 = rows_of(jnp.where(high, ROWS - 3, -1), (TILE, 1))
    last = column_step(get2, faces_of(get2), lambda k: links2[k], spin_of(row2))
    write_at = jnp.where(high, TILE - 2, 0)
    write = (sub >= write_at) & (sub < write_at + 2)
    for f in range(STATE):
        for k in range(LEVELS):
            x = jnp.where(high, roll(last[f][k], 5, 0), roll(last[f][k], -1, 0))
            (t_out, s_out, u_out, v_out)[f][k] = jnp.where(write, x, (t, s, u, v)[f][k])


def limit(mebibytes):
    return pltpu.CompilerParams(vmem_limit_bytes=mebibytes * 1024 * 1024)


def whole(shape):
    return pl.BlockSpec(shape, lambda *_: (0,) * len(shape))


def call(kernel, place, args, outs, scratch, mebibytes, flops, far_in=0, far_out=0):
    vmem, hbm = pl.BlockSpec(memory_space=pltpu.VMEM), pl.BlockSpec(memory_space=pltpu.HBM)
    args = [pltpu.with_memory_space_constraint(a, pltpu.HBM if i < far_in else pltpu.VMEM) for i, a in enumerate(args)]
    return pl.pallas_call(
        kernel,
        out_shape=[jax.ShapeDtypeStruct(o, F32) if i < far_out else pltpu.VMEM(o, F32) for i, o in enumerate(outs)],
        in_specs=[pl.BlockSpec(memory_space=pltpu.SMEM)] + [hbm if i < far_in else vmem for i in range(len(args))],
        out_specs=[hbm if i < far_out else vmem for i in range(len(outs))],
        scratch_shapes=[pltpu.VMEM(x, F32) if isinstance(x, tuple) else x for x in scratch],
        compiler_params=limit(mebibytes),
        cost_estimate=pl.CostEstimate(flops=flops, bytes_accessed=4_000_000, transcendentals=0),
    )(place, *args)


def edge_call(folds, place, own, got, inner, inner_ghost, fields):
    def block(shape, index):
        return pl.BlockSpec(shape, index)

    strip = pl.BlockSpec((LEVELS, TILE, COLS), lambda i, p: (0, p[2] * (BLOCKS - 1), 0))
    return pl.pallas_call(
        lambda *refs: edge_kernel(folds, *refs),
        out_shape=[jax.ShapeDtypeStruct(x.shape, F32) for x in fields],
        grid_spec=pltpu.PrefetchScalarGridSpec(
            num_scalar_prefetch=1,
            grid=(1,),
            in_specs=[
                block((1, MESSAGE, COLS), lambda i, p: (p[2], 0, 0)),
                whole((MESSAGE, COLS)),
                block((1, FIELDS, LEVELS, TILE, COLS), lambda i, p: (p[2], 0, 0, 0, 0)),
                block((1, FIELDS, TILE, COLS), lambda i, p: (p[2], 0, 0, 0)),
            ] + [strip] * STATE,
            out_specs=[strip] * STATE,
            scratch_shapes=[pltpu.VMEM((MESSAGE, COLS), F32)] * 2,
        ),
        input_output_aliases={5 + f: f for f in range(STATE)},
        compiler_params=limit(16),
        cost_estimate=pl.CostEstimate(flops=2_000_000, bytes_accessed=2_000_000, transcendentals=0),
    )(place, own, got, inner, inner_ghost, *fields)


def device(lon, lat, lats, lons):
    return lon % lons * lats + lat


def body(t, s, u, v, flag, tally):
    lons, lats = lax.axis_size("lon"), lax.axis_size("lat")
    lat, lon = lax.axis_index("lat"), lax.axis_index("lon")
    side_x = lat % 2
    place = jnp.stack([lat, lon, side_x]).astype(jnp.int32)
    place_y = jnp.stack([lat, lon, 1 - side_x]).astype(jnp.int32)
    pairs_p, pairs_q, pairs_x, pairs_y = [], [], [], []
    for a in range(lats):
        for o in range(lons):
            here = device(o, a, lats, lons)
            pairs_p.append((here, device(o ^ 1, a, lats, lons)))
            pairs_q.append((here, device(o + 1 if o % 2 else o - 1, a, lats, lons)))
            pairs_y.append((here, device(o, a ^ 1, lats, lons)))
            next_lat = a + 1 if a % 2 else a - 1
            inside = 0 <= next_lat < lats
            pairs_x.append((here, device(o, next_lat, lats, lons) if inside else device(lons - 1 - o, a, lats, lons)))

    def send(x, pairs):
        return lax.ppermute(x, ("lon", "lat"), pairs)

    deep, tall, square = (LEVELS, ROWS, COLS), (LEVELS, TALL, COLS), (FIELDS, COLS, COLS)
    message = (MESSAGE, COLS)
    col_p, col_q, own_cols, rows, wet = call(
        pack_kernel, place, (t, s, u, v, flag, tally), [(PACK, COLS), (PACK, COLS), square, (2, EDGE_AT, COLS), tall],
        [(STATE,) + tall, pltpu.VMEM(deep, jnp.int32), pltpu.VMEM((ROWS, COLS), jnp.int32), pltpu.SemaphoreType.DMA((6,)), square],
        12, 1_000_000, far_in=6)
    got_p, got_q = send(col_p, pairs_p), send(col_q, pairs_q)
    field1, open_e, link, spin = call(
        first_kernel, place, (t, s, u, v, wet), [(STATE,) + tall, deep, (3,) + deep, (ROWS, COLS)],
        [(STATE,) + tall, (2,) + tall, pltpu.SemaphoreType.DMA((STATE,))], 12, 40_000_000, far_in=STATE)
    strip, ghost, own, to_x, to_y = call(
        spread_kernel, place, (got_p, got_q, own_cols, rows), [square, square, (2, MESSAGE, COLS), message, message],
        [square], 4, 1_000_000)
    got_x, got_y = send(to_x, pairs_x), send(to_y, pairs_y)
    *fields, inner, inner_ghost = call(
        second_kernel, place, (field1, wet, open_e, link, spin, strip, ghost),
        [deep] * STATE + [(2, FIELDS, LEVELS, TILE, COLS), (2, FIELDS, TILE, COLS)],
        [(STATE,) + tall, (STATE,) + deep, (STATE + 2, COLS, COLS), (STATE + 2, COLS, COLS), (STATE + 2,) + tall, deep,
         (2,) + tall,
         pltpu.SemaphoreType.DMA((STATE, BLOCKS))], 20, 50_000_000, far_out=STATE)
    fields = edge_call(False, place_y, own, got_y, inner, inner_ghost, fields)
    fields = edge_call(True, place, own, got_x, inner, inner_ghost, fields)
    return tuple(fields)


def solution(mesh):
    cut = P(None, "lat", "lon")
    return jax.shard_map(
        body,
        mesh=mesh,
        in_specs=(cut, cut, cut, cut, cut, P("lat", "lon")),
        out_specs=(cut, cut, cut, cut),
        check_vma=False,
    )
```

```python
import jax
import jax.numpy as jnp
from jax import lax
from jax.experimental import pallas as pl
from jax.experimental.pallas import tpu as pltpu
from jax.sharding import PartitionSpec as P

TIME_STEP = 0.2
KAPPA = 0.1
VISCOSITY = 0.1
VERTICAL = 0.5
GRAVITY = 0.2
THERMAL = 0.3
HALINE = 0.2
CORIOLIS = 0.5

LEVELS = 15
ROWS = 96
COLS = 128
TILE = 8
BLOCKS = ROWS // TILE
PAD = TILE
TALL = ROWS + 2 * PAD
FIELDS = 5
STATE = 4
GROUPS = STATE + 3
SIGNS = (1.0, 1.0, -1.0, -1.0, 1.0)
PACK = 16 * 2 * FIELDS
WET_AT = 8 * LEVELS
EDGE_AT = WET_AT + 32
MESSAGE = EDGE_AT + 16
F32 = jnp.float32


def roll(x, shift, axis):
    return pltpu.roll(x, shift % x.shape[axis], axis)


def iota(shape, axis):
    return lax.broadcasted_iota(jnp.int32, shape, axis)


def links_of(wet):
    out = []
    above, ratio = None, None
    for k in range(LEVELS):
        below = VERTICAL * wet[k] * wet[k + 1] if k < LEVELS - 1 else None
        pivot = 1.0 + (below if below is not None else 0.0)
        if above is not None:
            pivot = pivot + above - above * ratio
        inverse = 1.0 / pivot
        ratio = below * inverse if below is not None else None
        out.append((above, inverse, ratio))
        above = below
    return out


def column_step(get, faces, links, spin, west=None, south=None):
    mix = KAPPA
    half = 0.5 * GRAVITY * TIME_STEP
    done = [[], [], [], []]
    forward, loose = [], []
    east_sum = north_sum = None
    for k in range(LEVELS):
        w, oe, ow, on, os = faces(k)
        u, uE, uW, uN, uS = (get(2, k, 0, 0), get(2, k, 0, 1), get(2, k, 0, -1), get(2, k, 1, 0), get(2, k, -1, 0))
        v, vE, vW, vN, vS = (get(3, k, 0, 0), get(3, k, 0, 1), get(3, k, 0, -1), get(3, k, 1, 0), get(3, k, -1, 0))
        uNW, vSE = get(2, k, 1, -1), get(3, k, -1, 1)
        coef = []
        for speed, face in ((u, oe), (uW, ow), (v, on), (vS, os)):
            if face is None:
                coef.append(None)
                continue
            low = jnp.maximum(speed, 0.0) + mix
            coef.append((face * low, face * (low - speed)))
        tracers = []
        east, north = [], []
        for f in (0, 1):
            c, cE, cN = get(f, k, 0, 0), get(f, k, 0, 1), get(f, k, 1, 0)
            out_e = coef[0][0] * c - coef[0][1] * cE
            if west is None:
                out_e = out_e - (coef[1][0] * get(f, k, 0, -1) - coef[1][1] * c)
            out_n = coef[2][0] * c - coef[2][1] * cN
            out_s = south(f, k, out_n) if south else coef[3][0] * get(f, k, -1, 0) - coef[3][1] * c
            tracers.append((c - TIME_STEP * (out_n - out_s), out_e))
            east.append(cE - c)
            north.append(cN - c)
        loose.append(tracers)
        east_now = (half * HALINE) * east[1] - (half * THERMAL) * east[0]
        north_now = (half * HALINE) * north[1] - (half * THERMAL) * north[0]
        east_p = east_now if k == 0 else east_sum + east_now
        north_p = north_now if k == 0 else north_sum + north_now
        east_sum, north_sum = east_p + east_now, north_p + north_now
        turn = TIME_STEP * VISCOSITY
        done[2].append(oe * ((1.0 - 4.0 * turn) * u + spin * ((v + vS) + (vE + vSE)) - east_p
                             + turn * ((uE + uW) + (uN + uS))))
        done[3].append(on * ((1.0 - 4.0 * turn) * v - spin * ((u + uN) + (uW + uNW)) - north_p
                             + turn * ((vE + vW) + (vN + vS))))
    for k in range(LEVELS):
        w = faces(k)[0]
        up, inverse, _ = links(k)
        now = []
        for f in (0, 1):
            kept, out = loose[k][f]
            x = w * (kept - TIME_STEP * (out - west(f, k, out) if west else out))
            now.append((x + up * forward[-1][f]) * inverse if k else x * inverse)
        forward.append(now)
    for f in (0, 1):
        value = forward[-1][f]
        back = [value]
        for k in range(LEVELS - 2, -1, -1):
            value = forward[k][f] + links(k)[2] * value
            back.append(value)
        done[f] = back[::-1]
    return done


def spin_of(row_index):
    angle = jnp.pi * ((row_index + 0.5) / (8.0 * ROWS) - 0.3)
    return (0.25 * TIME_STEP * CORIOLIS) * jnp.sin(angle)


SHIFTS = {0: (), 1: (), 2: (1, -1), 3: (-1, 1), 4: ()}


def eager(shift, fields):
    held = {}
    count = len(fields)
    for f in range(count):
        for k in range(LEVELS):
            held[f, k, 0, 0] = fields[f][k]
    for dj, di in ((0, 1), (0, -1), (1, 0), (-1, 0)):
        for f in range(count):
            for k in range(LEVELS):
                held[f, k, dj, di] = shift(fields[f][k], dj, di)
    for f in (2, 3):
        dj, di = SHIFTS[f]
        for k in range(LEVELS):
            held[f, k, dj, di] = shift(held[f, k, 0, di], dj, 0)
    return lambda f, k, dj, di: held[f, k, dj, di]


def faces_of(get):
    def faces(k):
        w = get(4, k, 0, 0)
        return (w, w * get(4, k, 0, 1), w * get(4, k, 0, -1), w * get(4, k, 1, 0), w * get(4, k, -1, 0))

    return faces


def split3(x):
    a = x.astype(jnp.bfloat16)
    rest = x - a.astype(F32)
    b = rest.astype(jnp.bfloat16)
    return a, b, (rest - b.astype(F32)).astype(jnp.bfloat16)


def picked(terms, pick):
    return sum(jnp.dot(x, pick, preferred_element_type=F32) for x in terms)


def slide(slot, patterns):
    slot[...] = jnp.zeros(slot.shape, F32)
    p, lane = iota((TILE, COLS), 0), iota((TILE, COLS), 1)
    for i, moves in enumerate(patterns):
        hit = jnp.zeros((TILE, COLS), F32)
        for to, sources in moves.items():
            for source in sources:
                hit = jnp.where((lane == to) & (p == source), 1.0, hit)
        slot[120:128, COLS * i:COLS * i + COLS] = hit


def slid(slot, k):
    return slot[120 - 8 * k:248 - 8 * k, :].astype(jnp.bfloat16)


AROUND = {126: (0,), 127: (1,), 0: (2,), 1: (3,)}
NEXT1 = {127: (1,), 0: (6,)}
OWN1 = {0: (2,), 127: (5,)}
THIRD = {1: 0, 2: 3, 5: 4, 6: 7}


def with_third(moves):
    return {to: (p, THIRD[p]) for to, (p,) in moves.items()}


def rows_at(b):
    return pl.multiple_of(b * TILE + PAD, TILE)


def pack_kernel(place, t, s, u, v, flag, tally, col_p, col_q, own_cols, rows, wet, t_in, s_in, u_in, v_in, open_e,
                link, spin, held_flag, held_tally, sems, gathered):
    field = (t_in, s_in, u_in, v_in)
    odd = place[1] % 2 == 1
    lane = iota((TILE, COLS), 1)
    sub = iota((TILE, COLS), 0)
    group = jnp.where(lane % 8 < 4, lane // 8, -1)
    inside = pl.ds(PAD, ROWS)
    copies = [pltpu.make_async_copy(x, field[f].at[:, inside, :], sems.at[f]) for f, x in enumerate((t, s, u, v))]
    copies.append(pltpu.make_async_copy(flag, held_flag, sems.at[4]))
    copies.append(pltpu.make_async_copy(tally, held_tally, sems.at[5]))
    for f in (4, 5, 0, 1, 2, 3):
        copies[f].start()
    copies[4].wait()
    copies[5].wait()

    def face_block(b, carry):
        here = pl.ds(rows_at(b), TILE)
        src = pl.ds(pl.multiple_of(b * TILE, TILE), TILE)
        deep = held_tally[src, :]
        column = [jnp.where(k < deep, held_flag[k, src, :], 0).astype(F32) for k in range(LEVELS)]
        for k, w in enumerate(column):
            wet[k, here, :] = w
            open_e[k, src, :] = w * roll(w, COLS - 1, 1)
        for k, (up, inverse, ratio) in enumerate(links_of(column)):
            if up is not None:
                link[0, k, src, :] = up
            link[1, k, src, :] = inverse
            if ratio is not None:
                link[2, k, src, :] = ratio
        row = (place[0] * ROWS + b * TILE + iota((TILE, COLS), 0)).astype(F32)
        spin[src, :] = spin_of(row)
        return carry

    lax.fori_loop(0, BLOCKS, face_block, 0, unroll=3)
    for f in (4, 0, 1, 2, 3):
        if f < STATE:
            copies[f].wait()
        for b in range(BLOCKS):
            at = PAD + TILE * b
            out = jnp.zeros((TILE, COLS), F32)
            for k in range(LEVELS):
                x = (field[f] if f < STATE else wet)[k, at:at + TILE, :]
                out = jnp.where(group == k, roll(x, 8 * k + 2, 1), out)
            gathered[f, TILE * b:TILE * b + TILE, :] = out
        gathered[f, ROWS:COLS, :] = jnp.zeros((COLS - ROWS, COLS), F32)
    for f in range(FIELDS):
        own_cols[f] = gathered[f].T
    for side, first in ((0, PAD), (1, PAD + ROWS - 2)):
        for m in range(LEVELS + 4):
            parts = []
            for i in range(4):
                at = first - 2 * i
                if m < LEVELS:
                    parts.append(field[i][m, at:at + TILE, :])
                else:
                    k = min(4 * (m - LEVELS) + i, LEVELS - 1)
                    parts.append(wet[k, at:at + TILE, :])
            rows[side, TILE * m:TILE * m + TILE, :] = jnp.where(
                sub < 2, parts[0], jnp.where(sub < 4, parts[1], jnp.where(sub < 6, parts[2], parts[3])))
    for f in range(FIELDS):
        for c in range(2):
            last = own_cols[f, pl.ds(c, 16, stride=8), :]
            first = own_cols[f, pl.ds(2 + c, 16, stride=8), :]
            at = (2 * f + c) * 16
            col_p[at:at + 16, :] = jnp.where(odd, first, last)
            col_q[at:at + 16, :] = jnp.where(odd, last, first)


def spread_kernel(place, got_p, got_q, own_cols, rows, _, strip, ghost, own, to_x, to_y, turned):
    odd = place[1] % 2 == 1
    lat_odd = place[0] % 2 == 1
    fold = place[0] == 7
    for f in range(FIELDS):
        for c in range(2):
            at = (2 * f + c) * 16
            a, b = got_p[at:at + 16, :], got_q[at:at + 16, :]
            west, east = jnp.where(odd, a, b), jnp.where(odd, b, a)
            strip[f, pl.ds(c, 16, stride=8), :] = west
            strip[f, pl.ds(6 + c, 16, stride=8), :] = east
            strip[f, pl.ds(2 + c, 16, stride=8), :] = own_cols[f, pl.ds(2 + c, 16, stride=8), :]
            strip[f, pl.ds(4 + c, 16, stride=8), :] = own_cols[f, pl.ds(c, 16, stride=8), :]
            turned[f, pl.ds(c, 16, stride=8), :] = west
            turned[f, pl.ds(2 + c, 16, stride=8), :] = east
            turned[f, pl.ds(4 + c, 16, stride=8), :] = west
            turned[f, pl.ds(6 + c, 16, stride=8), :] = east
    for f in range(FIELDS):
        ghost[f] = turned[f].T
    for f in range(FIELDS):
        own[0, EDGE_AT + 2 * f:EDGE_AT + 2 * f + 2, :] = ghost[f, 0:2, :]
        own[1, EDGE_AT + 2 * f:EDGE_AT + 2 * f + 2, :] = ghost[f, ROWS - 2:ROWS, :]
    for side in range(2):
        own[side, 0:EDGE_AT, :] = rows[side]
        own[side, EDGE_AT + 2 * FIELDS:MESSAGE, :] = jnp.zeros((MESSAGE - EDGE_AT - 2 * FIELDS, COLS), F32)
    low, high = own[0], own[1]
    to_x[...] = jnp.where(lat_odd, high, low)
    to_y[...] = jnp.where(lat_odd, low, high)

    @pl.when(fold)
    def _():
        a, b = iota((COLS, COLS), 0), iota((COLS, COLS), 1)
        mirror = (a + b == COLS - 1).astype(jnp.bfloat16)
        mirror_edge = ((a // 8 == b // 8) & (a % 8 < 4) & (a % 8 + b % 8 == 3)).astype(jnp.bfloat16)
        to_x[0:EDGE_AT, :] = picked(split3(own[1, 0:EDGE_AT, :]), mirror)
        to_x[EDGE_AT:MESSAGE, :] = picked(split3(own[1, EDGE_AT:MESSAGE, :]), mirror_edge)


def first_kernel(t, s, u, v, wet, open_e, link, spin, field1, flux):
    field = (t, s, u, v)

    def step_block(b, carry):
        r = rows_at(b)
        src = pl.ds(pl.multiple_of(b * TILE, TILE), TILE)

        def get(f, k, dj, di):
            x = field[f][k, pl.ds(r + dj, TILE), :]
            return roll(x, -di, 1) if di else x

        def faces(k):
            w = wet[k, pl.ds(r, TILE), :]
            return (w, open_e[k, src, :], None, w * wet[k, pl.ds(r + 1, TILE), :], None)

        def south(f, k, x):
            flux[f, k, pl.ds(r, TILE), :] = x
            return flux[f, k, pl.ds(r - 1, TILE), :]

        moved = column_step(get, faces, lambda k: tuple(link[i, k, src, :] for i in range(3)), spin[src, :],
                            lambda f, k, x: roll(x, 1, 1), south)
        for f in range(STATE):
            for k in range(LEVELS):
                field1[f, k, pl.ds(r, TILE), :] = moved[f][k]
        return carry

    lax.fori_loop(0, BLOCKS, step_block, 0, unroll=4)


def second_kernel(place, field1, wet, open_e, link, spin, strip, ghost, t, s, u, v, inner, inner_ghost, blocks,
                  state, outs, ghost1, turned, beside, face, flux, slot, slot_third, terms, sems):
    first_row = place[0] * ROWS
    lane = iota((TILE, COLS), 1)
    sub = iota((TILE, COLS), 0)

    def strip_shift(x, dj, di):
        if di:
            x = roll(x, -di, 0)
        return roll(x, -dj, 1) if dj else x

    values = [[strip[f, 8 * k:8 * k + 8, :] for k in range(LEVELS)] for f in range(FIELDS)]
    get1 = eager(strip_shift, values)
    row = (first_row + iota((1, COLS), 1)).astype(F32)
    links1 = links_of(values[4])
    moved = column_step(get1, faces_of(get1), lambda k: links1[k], spin_of(row))
    for f in range(STATE):
        for k in range(LEVELS):
            turned[f, 8 * k:8 * k + 8, :] = moved[f][k]
    faces1 = faces_of(get1)
    for f in range(2):
        for k in range(LEVELS):
            c, speed, face_e = moved[f][k], moved[2][k], faces1(k)[1]
            low = jnp.maximum(speed, 0.0) + KAPPA
            turned[STATE + f, 8 * k:8 * k + 8, :] = roll(face_e * (low * c - (low - speed) * roll(c, -1, 0)), 5, 0)
    for k in range(LEVELS):
        w = values[4][k]
        turned[GROUPS - 1, 8 * k:8 * k + 8, :] = jnp.where(sub == 2, roll(w, 1, 0), roll(w, -1, 0))
    for g in range(GROUPS):
        turned[g, 8 * LEVELS:COLS, :] = jnp.zeros((COLS - 8 * LEVELS, COLS), F32)
    for g in range(GROUPS):
        ghost1[g] = turned[g].T

    inside = pl.ds(PAD, ROWS)
    wide = iota((ROWS, COLS), 1)
    edge_lane = (wide == 0) | (wide == COLS - 1)
    place_in = wide % 8
    second = (place_in == 1) | (place_in == 2) | (place_in == 5) | (place_in == 6)
    from_east = (place_in == 0) | (place_in == 4)
    slide(slot, (NEXT1, OWN1))
    slide(slot_third, (with_third(NEXT1), with_third(OWN1)))
    for g in range(GROUPS):
        x = ghost1[g, 0:ROWS, :]
        a = x.astype(jnp.bfloat16)
        rest = x - a.astype(F32)
        b = rest.astype(jnp.bfloat16).astype(F32)
        c = rest - b
        terms[ROWS * g:ROWS * g + ROWS, 0:COLS] = a
        terms[ROWS * g:ROWS * g + ROWS, COLS:2 * COLS] = jnp.where(
            second, b, jnp.where(from_east, roll(c, -1, 1), roll(c, 1, 1))).astype(jnp.bfloat16)
    for k in range(LEVELS):
        pick = jnp.concatenate([slid(slot, k), slid(slot_third, k)], axis=0)
        found = jnp.dot(terms[...], pick, preferred_element_type=F32)
        face[k] = found[ROWS * (GROUPS - 1):, COLS:]
        for f in range(STATE + 2):
            beside[f, k, inside, :] = found[ROWS * f:ROWS * f + ROWS, :COLS]
        for f in range(STATE):
            state[f, k, inside, :] = jnp.where(edge_lane, found[ROWS * f:ROWS * f + ROWS, COLS:], field1[f, k, inside, :])

    def copies(b):
        src = pl.ds(pl.multiple_of(b * TILE, TILE), TILE)
        return [pltpu.make_async_copy(outs.at[f, :, src, :], x.at[:, src, :], sems.at[f, b])
                for f, x in enumerate((t, s, u, v))]

    def step_block(b, carry):
        r = rows_at(b)
        src = pl.ds(pl.multiple_of(b * TILE, TILE), TILE)

        def get(f, k, dj, di):
            here = pl.ds(r + dj, TILE)
            x = state[f, k, here, :]
            if di == 0:
                return x
            return roll(jnp.where(lane == (0 if di > 0 else COLS - 1), beside[f, k, here, :], x), -di, 1)

        def faces(k):
            w = wet[k, pl.ds(r, TILE), :]
            across = w * face[k, src, :]
            return (w, jnp.where(lane == COLS - 1, across, open_e[k, src, :]), None,
                    w * wet[k, pl.ds(r + 1, TILE), :], None)

        def west(f, k, x):
            return jnp.where(lane == 0, beside[STATE + f, k, pl.ds(r, TILE), :], roll(x, 1, 1))

        def south(f, k, x):
            flux[f, k, pl.ds(r, TILE), :] = x
            return flux[f, k, pl.ds(r - 1, TILE), :]

        moved = column_step(get, faces, lambda k: tuple(link[i, k, src, :] for i in range(3)), spin[src, :], west, south)
        for f in range(STATE):
            for k in range(LEVELS):
                outs[f, k, src, :] = moved[f][k]
        @pl.when((b > 0) & (b < BLOCKS - 1))
        def _():
            for c in copies(b):
                c.start()

        return carry

    lax.fori_loop(0, BLOCKS, step_block, 0, unroll=4)

    for f in range(FIELDS):
        for k in range(LEVELS):
            src = state.at[f, k] if f < STATE else wet.at[k]
            inner[f, k] = jnp.where(sub < 4, src[PAD - 1:PAD + 7, :], src[PAD + 89:PAD + 97, :])
        edge = ghost1.at[f] if f < STATE else ghost.at[4]
        inner_ghost[f] = jnp.where(sub < 4, roll(edge[0:8, :], 1, 0), edge[89:97, :])
    for f in range(STATE):
        for side, first in ((0, 0), (1, ROWS - TILE)):
            blocks[side, f] = outs[f, :, first:first + TILE, :]

    def drain(b, carry):
        for c in copies(b):
            c.wait()
        return carry

    lax.fori_loop(1, BLOCKS - 1, drain, 0)


def edge_kernel(place, own, got_x, got_y, inner, inner_ghost, blocks, t, s, u, v, t_out, s_out, u_out, v_out,
                low, high, mine_low, mine_high, slot, ring, lead, moved1, ring2, lead2, final, sems):
    lat = place[0]
    odd = lat % 2 == 1
    fold = lat == 7
    sub = iota((TILE, COLS), 0)
    lane = iota((TILE, COLS), 1)
    tile = slice(PAD, PAD + TILE)
    body_rows = slice(PAD, PAD + MESSAGE)
    from_x, from_y = got_x[...], got_y[...]
    low[body_rows, :] = jnp.where(odd, from_y, jnp.where(lat == 0, 0.0, from_x))
    high[body_rows, :] = jnp.where(odd, from_x, from_y)
    mine_low[body_rows, :] = own[0]
    mine_high[body_rows, :] = own[1]
    slide(slot, (AROUND, NEXT1))

    def rows(ref, at, early):
        return ref[PAD + at - early:PAD + at - early + TILE, :]

    def where_of(f, k):
        return 8 * k + 2 * f if f < STATE else WET_AT + 2 * k

    def stack(at, sign):
        top = jnp.where(fold, sign * rows(high, at, 5), rows(high, at, 6))
        return jnp.where(sub < 2, rows(low, at, 0), jnp.where(
            sub < 4, rows(mine_low, at, 2), jnp.where(sub < 6, rows(mine_high, at, 4), top)))

    def stack_fold(at, sign):
        return jnp.where(sub < 2, rows(high, at, 0), sign * rows(mine_high, at, 1))

    def spreads(tiles):
        terms = split3(jnp.concatenate(tiles, axis=0))
        out = []
        for k in range(LEVELS):
            found = picked(terms, slid(slot, k))
            out.append([(found[TILE * i:TILE * i + TILE, :COLS], found[TILE * i:TILE * i + TILE, COLS:])
                        for i in range(len(tiles))])
        return out

    def ring_getter(build, edges, back):
        held = {}
        for f in range(FIELDS):
            for k in range(LEVELS):
                x, g = build(where_of(f, k), SIGNS[f]), edges[k][f][0]
                ring[f, k, tile, :COLS] = x
                ring[f, k, tile, COLS:] = g
                held[f, k, 0, 0] = (x, g)
        for f in range(FIELDS):
            for k in range(LEVELS):
                x, g = held[f, k, 0, 0]
                a, b = jnp.where(lane == 0, g, x), jnp.where(lane == 0, x, g)
                held[f, k, 0, back] = (roll(a, -1, 1), roll(b, -1, 1))
                a, b = jnp.where(lane == COLS - 1, g, x), jnp.where(lane == COLS - 1, x, g)
                held[f, k, 0, -back] = (roll(a, 1, 1), roll(b, 1, 1))
        for f, di in ((2, -1), (3, 1)):
            for k in range(LEVELS):
                x, g = held[f, k, 0, di]
                lead[f - 2, k, tile, :COLS] = x
                lead[f - 2, k, tile, COLS:] = g

        def get(f, k, dj, di):
            if dj == 0:
                return jnp.concatenate(held[f, k, 0, di], axis=1)
            ref = lead.at[f - 2, k] if di else ring.at[f, k]
            return ref[PAD + dj:PAD + dj + TILE, :]

        return get

    def one_step(get, row):
        links = links_of([get(4, k, 0, 0) for k in range(LEVELS)])
        return column_step(get, faces_of(get), lambda k: links[k], spin_of(row))

    def global_rows(low_row, high_row):
        i = iota((TILE, 1), 0)
        return (lat * ROWS + i + jnp.where(i < 4, low_row, high_row - 4)).astype(F32)

    near_tiles = [inner_ghost[f] for f in range(FIELDS)]
    placed = spreads([stack(EDGE_AT + 2 * f, SIGNS[f]) for f in range(FIELDS)] + near_tiles)
    first = one_step(ring_getter(stack, placed, 1), global_rows(-2, ROWS - 2))
    for f in range(STATE):
        for k in range(LEVELS):
            moved1[f, k, tile, :] = first[f][k]
    for k in range(LEVELS):
        moved1[STATE, k, tile, :] = ring[STATE, k, tile, :]

    @pl.when(fold)
    def _():
        edges = spreads([stack_fold(EDGE_AT + 2 * f, SIGNS[f]) for f in range(FIELDS)])
        row = jnp.full((TILE, 1), 8.0 * ROWS - 1.0, F32)
        mirror = one_step(ring_getter(stack_fold, edges, -1), row)
        wide = iota((TILE, 2 * COLS), 0)
        for f in range(STATE):
            for k in range(LEVELS):
                ring[f, k, tile, :] = mirror[f][k]
        for f in range(STATE):
            for k in range(LEVELS):
                moved1[f, k, tile, :] = jnp.where(
                    wide == 6, SIGNS[f] * ring[f, k, PAD - 5:PAD + 3, :], moved1[f, k, tile, :])

    held = {}
    ghosts = {}
    for f in range(FIELDS):
        for k in range(LEVELS):
            down, up = moved1[f, k, PAD + 1:PAD + 1 + TILE, :], moved1[f, k, PAD - 1:PAD - 1 + TILE, :]
            near = placed[k][FIELDS + f][1 if f < STATE else 0]
            both = [jnp.where(sub < 2, down[:, c], jnp.where(sub < 6, mid, up[:, c]))
                    for c, mid in ((slice(0, COLS), inner[f, k]), (slice(COLS, 2 * COLS), near))]
            held[f, k, 0, 0], ghosts[f, k] = both
            ring2[f, k, tile, :] = both[0]
    for f in range(FIELDS):
        for k in range(LEVELS):
            x, g = held[f, k, 0, 0], ghosts[f, k]
            held[f, k, 0, 1] = roll(jnp.where(lane == 0, g, x), -1, 1)
            held[f, k, 0, -1] = roll(jnp.where(lane == COLS - 1, g, x), 1, 1)
    for f, di in ((2, -1), (3, 1)):
        for k in range(LEVELS):
            lead2[f - 2, k, tile, :] = held[f, k, 0, di]

    def get2(f, k, dj, di):
        if dj == 0:
            return held[f, k, 0, di]
        ref = lead2.at[f - 2, k] if di else ring2.at[f, k]
        return ref[PAD + dj:PAD + dj + TILE, :]

    last = one_step(get2, global_rows(-1, ROWS - 3))
    for f in range(STATE):
        for k in range(LEVELS):
            ring2[f, k, tile, :] = last[f][k]
    for f in range(STATE):
        for k in range(LEVELS):
            final[0, f, k] = jnp.where(sub < 2, ring2[f, k, PAD + 1:PAD + 1 + TILE, :], blocks[0, f, k])
            final[1, f, k] = jnp.where(sub >= 6, ring2[f, k, PAD - 1:PAD - 1 + TILE, :], blocks[1, f, k])
    copies = [pltpu.make_async_copy(final.at[side, f], x.at[:, first_row:first_row + TILE, :], sems.at[side, f])
              for f, x in enumerate((t_out, s_out, u_out, v_out)) for side, first_row in ((0, 0), (1, ROWS - TILE))]
    for c in copies:
        c.start()
    for c in copies:
        c.wait()


def limit(mebibytes):
    return pltpu.CompilerParams(vmem_limit_bytes=mebibytes * 1024 * 1024)


def call(kernel, place, args, outs, scratch, mebibytes, flops, far_in=0, far_out=0, handed_on=0):
    far = [i < far_in or i >= len(args) - handed_on for i in range(len(args))]
    vmem, hbm = pl.BlockSpec(memory_space=pltpu.VMEM), pl.BlockSpec(memory_space=pltpu.HBM)
    args = [pltpu.with_memory_space_constraint(a, pltpu.HBM if there else pltpu.VMEM) for a, there in zip(args, far)]
    return pl.pallas_call(
        kernel,
        out_shape=[jax.ShapeDtypeStruct(o, F32) if i < far_out else pltpu.VMEM(o, F32) for i, o in enumerate(outs)],
        in_specs=[pl.BlockSpec(memory_space=pltpu.SMEM)] + [hbm if there else vmem for there in far],
        out_specs=[hbm if i < far_out else vmem for i in range(len(outs))],
        scratch_shapes=[pltpu.VMEM(x, F32) if isinstance(x, tuple) else x for x in scratch],
        input_output_aliases={1 + len(args) - handed_on + i: i for i in range(handed_on)},
        compiler_params=limit(mebibytes),
        cost_estimate=pl.CostEstimate(flops=flops, bytes_accessed=4_000_000, transcendentals=0),
    )(place, *args)


def device(lon, lat, lats, lons):
    return lon % lons * lats + lat


def body(t, s, u, v, flag, tally):
    lons, lats = lax.axis_size("lon"), lax.axis_size("lat")
    lat, lon = lax.axis_index("lat"), lax.axis_index("lon")
    place = jnp.stack([lat, lon]).astype(jnp.int32)
    pairs_p, pairs_q, pairs_x, pairs_y = [], [], [], []
    for a in range(lats):
        for o in range(lons):
            here = device(o, a, lats, lons)
            pairs_p.append((here, device(o ^ 1, a, lats, lons)))
            pairs_q.append((here, device(o + 1 if o % 2 else o - 1, a, lats, lons)))
            pairs_y.append((here, device(o, a ^ 1, lats, lons)))
            next_lat = a + 1 if a % 2 else a - 1
            inside = 0 <= next_lat < lats
            pairs_x.append((here, device(o, next_lat, lats, lons) if inside else device(lons - 1 - o, a, lats, lons)))

    def send(x, pairs):
        return lax.ppermute(x, ("lon", "lat"), pairs)

    edges = (2, STATE, LEVELS, TILE, COLS)
    deep, tall, square = (LEVELS, ROWS, COLS), (LEVELS, TALL, COLS), (FIELDS, COLS, COLS)
    message = (MESSAGE, COLS)
    col_p, col_q, own_cols, rows, wet, *padded, open_e, link, spin = call(
        pack_kernel, place, (t, s, u, v, flag, tally), [(PACK, COLS), (PACK, COLS), square, (2, EDGE_AT, COLS)] + [tall] * 5
        + [deep, (3,) + deep, (ROWS, COLS)], [pltpu.VMEM(deep, jnp.int32), pltpu.VMEM((ROWS, COLS), jnp.int32), pltpu.SemaphoreType.DMA((6,)), square],
        12, 1_000_000, far_in=6)
    got_p, got_q = send(col_p, pairs_p), send(col_q, pairs_q)
    field1, = call(lambda _, *refs: first_kernel(*refs), place, (*padded, wet, open_e, link, spin), [(STATE,) + tall],
                   [(2,) + tall], 12, 40_000_000)
    strip, ghost, own, to_x, to_y = call(
        spread_kernel, place, (got_p, got_q, own_cols, rows, field1), [square, square, (2, MESSAGE, COLS), message, message],
        [square], 4, 1_000_000)
    got_x, got_y = send(to_x, pairs_x), send(to_y, pairs_y)
    *fields, inner, inner_ghost, blocks = call(
        second_kernel, place, (field1, wet, open_e, link, spin, strip, ghost),
        [deep] * STATE + [(FIELDS, LEVELS, TILE, COLS), (FIELDS, TILE, COLS), edges],
        [(STATE,) + tall, (STATE,) + deep, (GROUPS, COLS, COLS), (GROUPS, COLS, COLS), (STATE + 2,) + tall, deep,
         (2,) + tall, (248, 2 * COLS), (248, 2 * COLS), pltpu.VMEM((GROUPS * ROWS, 2 * COLS), jnp.bfloat16),
         pltpu.SemaphoreType.DMA((STATE, BLOCKS))], 20, 50_000_000, far_out=STATE)
    near, wide = (FIELDS, LEVELS, 3 * TILE, COLS), (FIELDS, LEVELS, 3 * TILE, 2 * COLS)
    padded = (MESSAGE + 2 * PAD, COLS)
    return tuple(call(
        edge_kernel, place, (own, got_x, got_y, inner, inner_ghost, blocks, *fields), [deep] * STATE,
        [padded] * 4 + [(248, 2 * COLS), wide, (2,) + wide[1:], wide, near, (2,) + near[1:], edges,
                        pltpu.SemaphoreType.DMA((2, STATE))], 16, 2_000_000, far_out=STATE, handed_on=STATE))


def solution(mesh):
    cut = P(None, "lat", "lon")
    return jax.shard_map(
        body,
        mesh=mesh,
        in_specs=(cut, cut, cut, cut, cut, P("lat", "lon")),
        out_specs=(cut, cut, cut, cut),
        check_vma=False,
    )
```

```python
import jax
import jax.numpy as jnp
from jax import lax
from jax.experimental import pallas as pl
from jax.experimental.pallas import tpu as pltpu
from jax.sharding import PartitionSpec as P

TIME_STEP = 0.2
KAPPA = 0.1
VISCOSITY = 0.1
VERTICAL = 0.5
GRAVITY = 0.2
THERMAL = 0.3
HALINE = 0.2
CORIOLIS = 0.5

LEVELS = 15
ROWS = 96
COLS = 128
TILE = 8
BLOCKS = ROWS // TILE
PAD = TILE
TALL = ROWS + 2 * PAD
FIELDS = 5
STATE = 4
GROUPS = STATE + 3
SIGNS = (1.0, 1.0, -1.0, -1.0, 1.0)
PACK = 16 * 2 * FIELDS
WET_AT = 8 * LEVELS
EDGE_AT = WET_AT + 32
MESSAGE = EDGE_AT + 16
F32 = jnp.float32


def roll(x, shift, axis):
    return pltpu.roll(x, shift % x.shape[axis], axis)


def iota(shape, axis):
    return lax.broadcasted_iota(jnp.int32, shape, axis)


def links_of(wet):
    out = []
    above, ratio = None, None
    for k in range(LEVELS):
        below = VERTICAL * wet[k] * wet[k + 1] if k < LEVELS - 1 else None
        pivot = 1.0 + (below if below is not None else 0.0)
        if above is not None:
            pivot = pivot + above - above * ratio
        inverse = 1.0 / pivot
        ratio = below * inverse if below is not None else None
        out.append((above, inverse, ratio))
        above = below
    return out


def column_step(get, faces, links, spin, west=None, south=None, early=None):
    mix = KAPPA
    half = 0.5 * GRAVITY
    keep = (1.0 - 4.0 * TIME_STEP * VISCOSITY) / TIME_STEP
    done = [[], [], [], []]
    forward, loose = [], []
    east_sum = north_sum = None
    for k in range(LEVELS):
        w, oe, ow, on, os = faces(k)
        u, uE, uW, uN, uS = (get(2, k, 0, 0), get(2, k, 0, 1), get(2, k, 0, -1), get(2, k, 1, 0), get(2, k, -1, 0))
        v, vE, vW, vN, vS = (get(3, k, 0, 0), get(3, k, 0, 1), get(3, k, 0, -1), get(3, k, 1, 0), get(3, k, -1, 0))
        uNW, vSE = get(2, k, 1, -1), get(3, k, -1, 1)
        coef = []
        for speed, face in ((u, oe), (uW, ow), (v, on), (vS, os)):
            if face is None:
                coef.append(None)
                continue
            low = jnp.maximum(speed, 0.0) + mix
            coef.append((face * low, face * (low - speed)))
        tracers = []
        east, north = [], []
        for f in (0, 1):
            c, cE, cN = get(f, k, 0, 0), get(f, k, 0, 1), get(f, k, 1, 0)
            out_e = coef[0][0] * c - coef[0][1] * cE
            if west is None:
                out_e = out_e - (coef[1][0] * get(f, k, 0, -1) - coef[1][1] * c)
            out_n = coef[2][0] * c - coef[2][1] * cN
            out_s = south(f, k, out_n) if south else coef[3][0] * get(f, k, -1, 0) - coef[3][1] * c
            tracers.append((c - (out_n - out_s), out_e))
            east.append(cE - c)
            north.append(cN - c)
        loose.append(tracers)
        east_now = (half * HALINE) * east[1] - (half * THERMAL) * east[0]
        north_now = (half * HALINE) * north[1] - (half * THERMAL) * north[0]
        east_p = east_now if k == 0 else east_sum + east_now
        north_p = north_now if k == 0 else north_sum + north_now
        east_sum, north_sum = east_p + east_now, north_p + north_now
        done[2].append(oe * (keep * u + spin * ((v + vS) + (vE + vSE)) - east_p
                             + VISCOSITY * ((uE + uW) + (uN + uS))))
        done[3].append(on * (keep * v - spin * ((u + uN) + (uW + uNW)) - north_p
                             + VISCOSITY * ((vE + vW) + (vN + vS))))
    if early:
        early(done)
    for k in range(LEVELS):
        w = faces(k)[0]
        up, inverse, _ = links(k)
        now = []
        for f in (0, 1):
            kept, out = loose[k][f]
            x = w * (kept - (out - west(f, k, out) if west else out))
            now.append((x + up * forward[-1][f]) * inverse if k else x * inverse)
        forward.append(now)
    for f in (0, 1):
        value = forward[-1][f]
        back = [value]
        for k in range(LEVELS - 2, -1, -1):
            value = forward[k][f] + links(k)[2] * value
            back.append(value)
        done[f] = back[::-1]
    return done


def spin_of(row_index):
    angle = jnp.pi * ((row_index + 0.5) / (8.0 * ROWS) - 0.3)
    return (0.25 * CORIOLIS) * jnp.sin(angle)


SHIFTS = {0: (), 1: (), 2: (1, -1), 3: (-1, 1), 4: ()}


def eager(shift, fields):
    held = {}
    count = len(fields)
    for f in range(count):
        for k in range(LEVELS):
            held[f, k, 0, 0] = fields[f][k]
    for dj, di in ((0, 1), (0, -1), (1, 0), (-1, 0)):
        for f in range(count):
            for k in range(LEVELS):
                held[f, k, dj, di] = shift(fields[f][k], dj, di)
    for f in (2, 3):
        dj, di = SHIFTS[f]
        for k in range(LEVELS):
            held[f, k, dj, di] = shift(held[f, k, 0, di], dj, 0)
    return lambda f, k, dj, di: held[f, k, dj, di]


def faces_of(get):
    def faces(k):
        w = get(4, k, 0, 0)
        long = TIME_STEP * w
        return (w, long * get(4, k, 0, 1), long * get(4, k, 0, -1), long * get(4, k, 1, 0), long * get(4, k, -1, 0))

    return faces


def split3(x):
    a = x.astype(jnp.bfloat16)
    rest = x - a.astype(F32)
    b = rest.astype(jnp.bfloat16)
    return a, b, (rest - b.astype(F32)).astype(jnp.bfloat16)


def picked(terms, pick):
    return sum(jnp.dot(x, pick, preferred_element_type=F32) for x in terms)


def slide(slot, patterns):
    slot[...] = jnp.zeros(slot.shape, F32)
    p, lane = iota((TILE, COLS), 0), iota((TILE, COLS), 1)
    for i, moves in enumerate(patterns):
        hit = jnp.zeros((TILE, COLS), F32)
        for to, sources in moves.items():
            for source in sources:
                hit = jnp.where((lane == to) & (p == source), 1.0, hit)
        slot[120:128, COLS * i:COLS * i + COLS] = hit


def slid(slot, k):
    return slot[120 - 8 * k:248 - 8 * k, :].astype(jnp.bfloat16)


AROUND = {126: (0,), 127: (1,), 0: (2,), 1: (3,)}
NEXT1 = {127: (1,), 0: (6,)}
OWN1 = {0: (2,), 127: (5,)}
THIRD = {1: 0, 2: 3, 5: 4, 6: 7}


def with_third(moves):
    return {to: (p, THIRD[p]) for to, (p,) in moves.items()}


def pack_kernel(place, t, s, u, v, flag, tally, col_p, col_q, own_cols, rows, wet, t_in, s_in, u_in, v_in, open_e,
                link, spin, held_flag, held_tally, sems, gathered):
    field = (t_in, s_in, u_in, v_in)
    odd = place[1] % 2 == 1
    lane = iota((TILE, COLS), 1)
    sub = iota((TILE, COLS), 0)
    group = jnp.where(lane % 8 < 4, lane // 8, -1)
    inside = pl.ds(PAD, ROWS)
    copies = [pltpu.make_async_copy(x, field[f].at[:, inside, :], sems.at[f]) for f, x in enumerate((t, s, u, v))]
    copies.append(pltpu.make_async_copy(flag, held_flag, sems.at[4]))
    copies.append(pltpu.make_async_copy(tally, held_tally, sems.at[5]))
    for f in (4, 5, 0, 1, 2, 3):
        copies[f].start()
    copies[4].wait()
    copies[5].wait()

    def gather(f, b):
        at = PAD + TILE * b
        out = jnp.zeros((TILE, COLS), F32)
        for k in range(LEVELS):
            x = (field[f] if f < STATE else wet)[k, at:at + TILE, :]
            out = jnp.where(group == k, roll(x, 8 * k + 2, 1), out)
        gathered[f, TILE * b:TILE * b + TILE, :] = out

    def couple(b):
        here = slice(TILE * b, TILE * b + TILE)
        column = [wet[k, PAD + TILE * b:PAD + TILE * b + TILE, :] for k in range(LEVELS)]
        for k, w in enumerate(column):
            open_e[k, here, :] = (TIME_STEP * w) * roll(w, COLS - 1, 1)
        for k, (up, inverse, ratio) in enumerate(links_of(column)):
            if up is not None:
                link[0, k, here, :] = up
            link[1, k, here, :] = inverse
            if ratio is not None:
                link[2, k, here, :] = ratio
        row = (place[0] * ROWS + b * TILE + iota((TILE, COLS), 0)).astype(F32)
        spin[here, :] = spin_of(row)

    for b in range(BLOCKS):
        here = slice(TILE * b, TILE * b + TILE)
        deep = held_tally[here, :]
        for k in range(LEVELS):
            wet[k, PAD + TILE * b:PAD + TILE * b + TILE, :] = jnp.where(k < deep, held_flag[k, here, :], 0).astype(F32)
    for f in (4, 0, 1, 2, 3):
        if f < STATE:
            copies[f].wait()
        for b in range(BLOCKS):
            gather(f, b)
            if f != 3 and b % 4 == 3:
                couple(3 * (0 if f == 4 else f + 1) + b // 4)
        gathered[f, ROWS:COLS, :] = jnp.zeros((COLS - ROWS, COLS), F32)
    for f in range(FIELDS):
        own_cols[f] = gathered[f].T
    for side, first in ((0, PAD), (1, PAD + ROWS - 2)):
        for m in range(LEVELS + 4):
            parts = []
            for i in range(4):
                at = first - 2 * i
                if m < LEVELS:
                    parts.append(field[i][m, at:at + TILE, :])
                else:
                    k = min(4 * (m - LEVELS) + i, LEVELS - 1)
                    parts.append(wet[k, at:at + TILE, :])
            rows[side, TILE * m:TILE * m + TILE, :] = jnp.where(
                sub < 2, parts[0], jnp.where(sub < 4, parts[1], jnp.where(sub < 6, parts[2], parts[3])))
    for f in range(FIELDS):
        for c in range(2):
            last = own_cols[f, pl.ds(c, 16, stride=8), :]
            first = own_cols[f, pl.ds(2 + c, 16, stride=8), :]
            at = (2 * f + c) * 16
            col_p[at:at + 16, :] = jnp.where(odd, first, last)
            col_q[at:at + 16, :] = jnp.where(odd, last, first)


def spread_kernel(place, got_p, got_q, own_cols, rows, _, strip, ghost, own, to_x, to_y, turned):
    odd = place[1] % 2 == 1
    lat_odd = place[0] % 2 == 1
    fold = place[0] == 7
    for f in range(FIELDS):
        for c in range(2):
            at = (2 * f + c) * 16
            a, b = got_p[at:at + 16, :], got_q[at:at + 16, :]
            west, east = jnp.where(odd, a, b), jnp.where(odd, b, a)
            strip[f, pl.ds(c, 16, stride=8), :] = west
            strip[f, pl.ds(6 + c, 16, stride=8), :] = east
            strip[f, pl.ds(2 + c, 16, stride=8), :] = own_cols[f, pl.ds(2 + c, 16, stride=8), :]
            strip[f, pl.ds(4 + c, 16, stride=8), :] = own_cols[f, pl.ds(c, 16, stride=8), :]
            turned[f, pl.ds(c, 16, stride=8), :] = west
            turned[f, pl.ds(2 + c, 16, stride=8), :] = east
            turned[f, pl.ds(4 + c, 16, stride=8), :] = west
            turned[f, pl.ds(6 + c, 16, stride=8), :] = east
    for f in range(FIELDS):
        ghost[f] = turned[f].T
    for f in range(FIELDS):
        own[0, EDGE_AT + 2 * f:EDGE_AT + 2 * f + 2, :] = ghost[f, 0:2, :]
        own[1, EDGE_AT + 2 * f:EDGE_AT + 2 * f + 2, :] = ghost[f, ROWS - 2:ROWS, :]
    for side in range(2):
        own[side, 0:EDGE_AT, :] = rows[side]
        own[side, EDGE_AT + 2 * FIELDS:MESSAGE, :] = jnp.zeros((MESSAGE - EDGE_AT - 2 * FIELDS, COLS), F32)
    low, high = own[0], own[1]
    to_x[...] = jnp.where(lat_odd, high, low)
    to_y[...] = jnp.where(lat_odd, low, high)

    @pl.when(fold)
    def _():
        a, b = iota((COLS, COLS), 0), iota((COLS, COLS), 1)
        mirror = (a + b == COLS - 1).astype(jnp.bfloat16)
        mirror_edge = ((a // 8 == b // 8) & (a % 8 < 4) & (a % 8 + b % 8 == 3)).astype(jnp.bfloat16)
        to_x[0:EDGE_AT, :] = picked(split3(own[1, 0:EDGE_AT, :]), mirror)
        to_x[EDGE_AT:MESSAGE, :] = picked(split3(own[1, EDGE_AT:MESSAGE, :]), mirror_edge)


def first_kernel(t, s, u, v, wet, open_e, link, spin, field1, flux):
    field = (t, s, u, v)

    def step_block(b):
        r = PAD + TILE * b
        src = slice(TILE * b, TILE * b + TILE)

        def get(f, k, dj, di):
            x = field[f][k, r + dj:r + dj + TILE, :]
            return roll(x, -di, 1) if di else x

        def faces(k):
            w = wet[k, r:r + TILE, :]
            return (w, open_e[k, src, :], None, (TIME_STEP * w) * wet[k, r + 1:r + 1 + TILE, :], None)

        def south(f, k, x):
            flux[f, k, r:r + TILE, :] = x
            return flux[f, k, r - 1:r - 1 + TILE, :]

        moved = column_step(get, faces, lambda k: tuple(link[i, k, src, :] for i in range(3)), spin[src, :],
                            lambda f, k, x: roll(x, 1, 1), south)
        for f in range(STATE):
            for k in range(LEVELS):
                field1[f, k, r:r + TILE, :] = moved[f][k]

    for b in range(BLOCKS):
        step_block(b)


def second_kernel(place, field1, wet, open_e, link, spin, strip, ghost, t, s, u, v, inner, inner_ghost, blocks,
                  state, outs, ghost1, turned, beside, face, flux, slot, slot_third, terms, sems):
    first_row = place[0] * ROWS
    lane = iota((TILE, COLS), 1)
    sub = iota((TILE, COLS), 0)

    def strip_shift(x, dj, di):
        if di:
            x = roll(x, -di, 0)
        return roll(x, -dj, 1) if dj else x

    values = [[strip[f, 8 * k:8 * k + 8, :] for k in range(LEVELS)] for f in range(FIELDS)]
    get1 = eager(strip_shift, values)
    row = (first_row + iota((1, COLS), 1)).astype(F32)
    links1 = links_of(values[4])
    moved = column_step(get1, faces_of(get1), lambda k: links1[k], spin_of(row))
    for f in range(STATE):
        for k in range(LEVELS):
            turned[f, 8 * k:8 * k + 8, :] = moved[f][k]
    faces1 = faces_of(get1)
    for f in range(2):
        for k in range(LEVELS):
            c, speed, face_e = moved[f][k], moved[2][k], faces1(k)[1]
            low = jnp.maximum(speed, 0.0) + KAPPA
            turned[STATE + f, 8 * k:8 * k + 8, :] = roll(face_e * (low * c - (low - speed) * roll(c, -1, 0)), 5, 0)
    for k in range(LEVELS):
        w = values[4][k]
        turned[GROUPS - 1, 8 * k:8 * k + 8, :] = jnp.where(sub == 2, roll(w, 1, 0), roll(w, -1, 0))
    for g in range(GROUPS):
        turned[g, 8 * LEVELS:COLS, :] = jnp.zeros((COLS - 8 * LEVELS, COLS), F32)
    for g in range(GROUPS):
        ghost1[g] = turned[g].T

    inside = pl.ds(PAD, ROWS)
    wide = iota((ROWS, COLS), 1)
    edge_lane = (wide == 0) | (wide == COLS - 1)
    place_in = wide % 8
    second = (place_in == 1) | (place_in == 2) | (place_in == 5) | (place_in == 6)
    from_east = (place_in == 0) | (place_in == 4)
    slide(slot, (NEXT1, OWN1))
    slide(slot_third, (with_third(NEXT1), with_third(OWN1)))
    for g in range(GROUPS):
        x = ghost1[g, 0:ROWS, :]
        a = x.astype(jnp.bfloat16)
        rest = x - a.astype(F32)
        b = rest.astype(jnp.bfloat16).astype(F32)
        c = rest - b
        terms[ROWS * g:ROWS * g + ROWS, 0:COLS] = a
        terms[ROWS * g:ROWS * g + ROWS, COLS:2 * COLS] = jnp.where(
            second, b, jnp.where(from_east, roll(c, -1, 1), roll(c, 1, 1))).astype(jnp.bfloat16)
    for k in range(LEVELS):
        pick = jnp.concatenate([slid(slot, k), slid(slot_third, k)], axis=0)
        found = jnp.dot(terms[...], pick, preferred_element_type=F32)
        face[k] = found[ROWS * (GROUPS - 1):, COLS:]
        for f in range(STATE + 2):
            beside[f, k, inside, :] = found[ROWS * f:ROWS * f + ROWS, :COLS]
        for f in range(STATE):
            state[f, k, inside, :] = jnp.where(edge_lane, found[ROWS * f:ROWS * f + ROWS, COLS:], field1[f, k, inside, :])

    def copies(b):
        src = slice(TILE * b, TILE * b + TILE)
        return [pltpu.make_async_copy(outs.at[f, :, src, :], x.at[:, src, :], sems.at[f, b])
                for f, x in enumerate((t, s, u, v))]

    def step_block(b):
        r = PAD + TILE * b
        src = slice(TILE * b, TILE * b + TILE)

        def get(f, k, dj, di):
            here = slice(r + dj, r + dj + TILE)
            x = state[f, k, here, :]
            if di == 0:
                return x
            return roll(jnp.where(lane == (0 if di > 0 else COLS - 1), beside[f, k, here, :], x), -di, 1)

        def faces(k):
            w = wet[k, r:r + TILE, :]
            long = TIME_STEP * w
            return (w, jnp.where(lane == COLS - 1, long * face[k, src, :], open_e[k, src, :]), None,
                    long * wet[k, r + 1:r + 1 + TILE, :], None)

        def west(f, k, x):
            return jnp.where(lane == 0, beside[STATE + f, k, r:r + TILE, :], roll(x, 1, 1))

        def south(f, k, x):
            flux[f, k, r:r + TILE, :] = x
            return flux[f, k, r - 1:r - 1 + TILE, :]

        moved = column_step(get, faces, lambda k: tuple(link[i, k, src, :] for i in range(3)), spin[src, :], west, south)
        for f in range(STATE):
            for k in range(LEVELS):
                if 0 < b < BLOCKS - 1:
                    outs[f, k, src, :] = moved[f][k]
                else:
                    blocks[b // (BLOCKS - 1), f, k] = moved[f][k]
        if 0 < b < BLOCKS - 1:
            for c in copies(b):
                c.start()

    for b in range(BLOCKS):
        step_block(b)

    for f in range(FIELDS):
        for k in range(LEVELS):
            src = state.at[f, k] if f < STATE else wet.at[k]
            inner[f, k] = jnp.where(sub < 4, src[PAD - 1:PAD + 7, :], src[PAD + 89:PAD + 97, :])
        edge = ghost1.at[f] if f < STATE else ghost.at[4]
        inner_ghost[f] = jnp.where(sub < 4, roll(edge[0:8, :], 1, 0), edge[89:97, :])
    for b in range(1, BLOCKS - 1):
        for c in copies(b):
            c.wait()


def edge_kernel(place, own, got_x, got_y, inner, inner_ghost, blocks, t, s, u, v, t_out, s_out, u_out, v_out,
                low, high, mine_low, mine_high, slot, ring, lead, moved1, ring2, lead2, final, sems):
    lat = place[0]
    odd = lat % 2 == 1
    fold = lat == 7
    sub = iota((TILE, COLS), 0)
    lane = iota((TILE, COLS), 1)
    tile = slice(PAD, PAD + TILE)
    body_rows = slice(PAD, PAD + MESSAGE)
    from_x, from_y = got_x[...], got_y[...]
    low[body_rows, :] = jnp.where(odd, from_y, jnp.where(lat == 0, 0.0, from_x))
    high[body_rows, :] = jnp.where(odd, from_x, from_y)
    mine_low[body_rows, :] = own[0]
    mine_high[body_rows, :] = own[1]
    slide(slot, (AROUND, NEXT1))

    def rows(ref, at, early):
        return ref[PAD + at - early:PAD + at - early + TILE, :]

    def where_of(f, k):
        return 8 * k + 2 * f if f < STATE else WET_AT + 2 * k

    def stack(at, sign):
        top = jnp.where(fold, sign * rows(high, at, 5), rows(high, at, 6))
        return jnp.where(sub < 2, rows(low, at, 0), jnp.where(
            sub < 4, rows(mine_low, at, 2), jnp.where(sub < 6, rows(mine_high, at, 4), top)))

    def stack_fold(at, sign):
        return jnp.where(sub < 2, rows(high, at, 0), sign * rows(mine_high, at, 1))

    def spreads(tiles):
        terms = split3(jnp.concatenate(tiles, axis=0))
        out = []
        for k in range(LEVELS):
            found = picked(terms, slid(slot, k))
            out.append([(found[TILE * i:TILE * i + TILE, :COLS], found[TILE * i:TILE * i + TILE, COLS:])
                        for i in range(len(tiles))])
        return out

    def ring_getter(build, edges, back):
        held = {}
        for f in range(FIELDS):
            for k in range(LEVELS):
                x, g = build(where_of(f, k), SIGNS[f]), edges[k][f][0]
                ring[f, k, tile, :COLS] = x
                ring[f, k, tile, COLS:] = g
                held[f, k, 0, 0] = (x, g)
        for f in range(FIELDS):
            for k in range(LEVELS):
                x, g = held[f, k, 0, 0]
                a, b = jnp.where(lane == 0, g, x), jnp.where(lane == 0, x, g)
                held[f, k, 0, back] = (roll(a, -1, 1), roll(b, -1, 1))
                a, b = jnp.where(lane == COLS - 1, g, x), jnp.where(lane == COLS - 1, x, g)
                held[f, k, 0, -back] = (roll(a, 1, 1), roll(b, 1, 1))
        for f, di in ((2, -1), (3, 1)):
            for k in range(LEVELS):
                x, g = held[f, k, 0, di]
                lead[f - 2, k, tile, :COLS] = x
                lead[f - 2, k, tile, COLS:] = g

        def get(f, k, dj, di):
            if dj == 0:
                return jnp.concatenate(held[f, k, 0, di], axis=1)
            ref = lead.at[f - 2, k] if di else ring.at[f, k]
            return ref[PAD + dj:PAD + dj + TILE, :]

        return get

    def one_step(get, row, early=None):
        links = links_of([get(4, k, 0, 0) for k in range(LEVELS)])
        return column_step(get, faces_of(get), lambda k: links[k], spin_of(row), early=early)

    def global_rows(low_row, high_row):
        i = iota((TILE, 1), 0)
        return (lat * ROWS + i + jnp.where(i < 4, low_row, high_row - 4)).astype(F32)

    near_tiles = [inner_ghost[f] for f in range(FIELDS)]
    placed = spreads([stack(EDGE_AT + 2 * f, SIGNS[f]) for f in range(FIELDS)] + near_tiles)
    first = one_step(ring_getter(stack, placed, 1), global_rows(-2, ROWS - 2))
    for f in range(STATE):
        for k in range(LEVELS):
            moved1[f, k, tile, :] = first[f][k]
    for k in range(LEVELS):
        moved1[STATE, k, tile, :] = ring[STATE, k, tile, :]

    @pl.when(fold)
    def _():
        edges = spreads([stack_fold(EDGE_AT + 2 * f, SIGNS[f]) for f in range(FIELDS)])
        row = jnp.full((TILE, 1), 8.0 * ROWS - 1.0, F32)
        mirror = one_step(ring_getter(stack_fold, edges, -1), row)
        wide = iota((TILE, 2 * COLS), 0)
        for f in range(STATE):
            for k in range(LEVELS):
                ring[f, k, tile, :] = mirror[f][k]
        for f in range(STATE):
            for k in range(LEVELS):
                moved1[f, k, tile, :] = jnp.where(
                    wide == 6, SIGNS[f] * ring[f, k, PAD - 5:PAD + 3, :], moved1[f, k, tile, :])

    held = {}
    ghosts = {}
    for f in range(FIELDS):
        for k in range(LEVELS):
            down, up = moved1[f, k, PAD + 1:PAD + 1 + TILE, :], moved1[f, k, PAD - 1:PAD - 1 + TILE, :]
            near = placed[k][FIELDS + f][1 if f < STATE else 0]
            both = [jnp.where(sub < 2, down[:, c], jnp.where(sub < 6, mid, up[:, c]))
                    for c, mid in ((slice(0, COLS), inner[f, k]), (slice(COLS, 2 * COLS), near))]
            held[f, k, 0, 0], ghosts[f, k] = both
            ring2[f, k, tile, :] = both[0]
    for f in range(FIELDS):
        for k in range(LEVELS):
            x, g = held[f, k, 0, 0], ghosts[f, k]
            held[f, k, 0, 1] = roll(jnp.where(lane == 0, g, x), -1, 1)
            held[f, k, 0, -1] = roll(jnp.where(lane == COLS - 1, g, x), 1, 1)
    for f, di in ((2, -1), (3, 1)):
        for k in range(LEVELS):
            lead2[f - 2, k, tile, :] = held[f, k, 0, di]

    def get2(f, k, dj, di):
        if dj == 0:
            return held[f, k, 0, di]
        ref = lead2.at[f - 2, k] if di else ring2.at[f, k]
        return ref[PAD + dj:PAD + dj + TILE, :]

    def finish(f, levels):
        for k in range(LEVELS):
            ring2[f, k, tile, :] = levels[k]
        for k in range(LEVELS):
            final[0, f, k] = jnp.where(sub < 2, ring2[f, k, PAD + 1:PAD + 1 + TILE, :], blocks[0, f, k])
            final[1, f, k] = jnp.where(sub >= 6, ring2[f, k, PAD - 1:PAD - 1 + TILE, :], blocks[1, f, k])
        x = (t_out, s_out, u_out, v_out)[f]
        copies = [pltpu.make_async_copy(final.at[side, f], x.at[:, first_row:first_row + TILE, :], sems.at[side, f])
                  for side, first_row in ((0, 0), (1, ROWS - TILE))]
        for c in copies:
            c.start()
        return copies

    flying = []

    def early(done):
        for f in (2, 3):
            flying.extend(finish(f, done[f]))

    last = one_step(get2, global_rows(-1, ROWS - 3), early)
    for f in (0, 1):
        flying.extend(finish(f, last[f]))
    for c in flying:
        c.wait()


def limit(mebibytes):
    return pltpu.CompilerParams(vmem_limit_bytes=mebibytes * 1024 * 1024)


def call(kernel, place, args, outs, scratch, mebibytes, flops, far_in=0, far_out=0, handed_on=0):
    far = [i < far_in or i >= len(args) - handed_on for i in range(len(args))]
    vmem, hbm = pl.BlockSpec(memory_space=pltpu.VMEM), pl.BlockSpec(memory_space=pltpu.HBM)
    args = [pltpu.with_memory_space_constraint(a, pltpu.HBM if there else pltpu.VMEM) for a, there in zip(args, far)]
    return pl.pallas_call(
        kernel,
        out_shape=[jax.ShapeDtypeStruct(o, F32) if i < far_out else pltpu.VMEM(o, F32) for i, o in enumerate(outs)],
        in_specs=[pl.BlockSpec(memory_space=pltpu.SMEM)] + [hbm if there else vmem for there in far],
        out_specs=[hbm if i < far_out else vmem for i in range(len(outs))],
        scratch_shapes=[pltpu.VMEM(x, F32) if isinstance(x, tuple) else x for x in scratch],
        input_output_aliases={1 + len(args) - handed_on + i: i for i in range(handed_on)},
        compiler_params=limit(mebibytes),
        cost_estimate=pl.CostEstimate(flops=flops, bytes_accessed=4_000_000, transcendentals=0),
    )(place, *args)


def device(lon, lat, lats, lons):
    return lon % lons * lats + lat


def body(t, s, u, v, flag, tally):
    lons, lats = lax.axis_size("lon"), lax.axis_size("lat")
    lat, lon = lax.axis_index("lat"), lax.axis_index("lon")
    place = jnp.stack([lat, lon]).astype(jnp.int32)
    pairs_p, pairs_q, pairs_x, pairs_y = [], [], [], []
    for a in range(lats):
        for o in range(lons):
            here = device(o, a, lats, lons)
            pairs_p.append((here, device(o ^ 1, a, lats, lons)))
            pairs_q.append((here, device(o + 1 if o % 2 else o - 1, a, lats, lons)))
            pairs_y.append((here, device(o, a ^ 1, lats, lons)))
            next_lat = a + 1 if a % 2 else a - 1
            inside = 0 <= next_lat < lats
            pairs_x.append((here, device(o, next_lat, lats, lons) if inside else device(lons - 1 - o, a, lats, lons)))

    def send(x, pairs):
        return lax.ppermute(x, ("lon", "lat"), pairs)

    edges = (2, STATE, LEVELS, TILE, COLS)
    deep, tall, square = (LEVELS, ROWS, COLS), (LEVELS, TALL, COLS), (FIELDS, COLS, COLS)
    message = (MESSAGE, COLS)
    col_p, col_q, own_cols, rows, wet, *padded, open_e, link, spin = call(
        pack_kernel, place, (t, s, u, v, flag, tally), [(PACK, COLS), (PACK, COLS), square, (2, EDGE_AT, COLS)] + [tall] * 5
        + [deep, (3,) + deep, (ROWS, COLS)], [pltpu.VMEM(deep, jnp.int32), pltpu.VMEM((ROWS, COLS), jnp.int32), pltpu.SemaphoreType.DMA((6,)), square],
        12, 1_000_000, far_in=6)
    got_p, got_q = send(col_p, pairs_p), send(col_q, pairs_q)
    field1, = call(lambda _, *refs: first_kernel(*refs), place, (*padded, wet, open_e, link, spin), [(STATE,) + tall],
                   [(2,) + tall], 12, 40_000_000)
    strip, ghost, own, to_x, to_y = call(
        spread_kernel, place, (got_p, got_q, own_cols, rows, field1), [square, square, (2, MESSAGE, COLS), message, message],
        [square], 4, 1_000_000)
    got_x, got_y = send(to_x, pairs_x), send(to_y, pairs_y)
    *fields, inner, inner_ghost, blocks = call(
        second_kernel, place, (field1, wet, open_e, link, spin, strip, ghost),
        [deep] * STATE + [(FIELDS, LEVELS, TILE, COLS), (FIELDS, TILE, COLS), edges],
        [(STATE,) + tall, (STATE,) + deep, (GROUPS, COLS, COLS), (GROUPS, COLS, COLS), (STATE + 2,) + tall, deep,
         (2,) + tall, (248, 2 * COLS), (248, 2 * COLS), pltpu.VMEM((GROUPS * ROWS, 2 * COLS), jnp.bfloat16),
         pltpu.SemaphoreType.DMA((STATE, BLOCKS))], 20, 50_000_000, far_out=STATE)
    near, wide = (FIELDS, LEVELS, 3 * TILE, COLS), (FIELDS, LEVELS, 3 * TILE, 2 * COLS)
    padded = (MESSAGE + 2 * PAD, COLS)
    return tuple(call(
        edge_kernel, place, (own, got_x, got_y, inner, inner_ghost, blocks, *fields), [deep] * STATE,
        [padded] * 4 + [(248, 2 * COLS), wide, (2,) + wide[1:], wide, near, (2,) + near[1:], edges,
                        pltpu.SemaphoreType.DMA((2, STATE))], 16, 2_000_000, far_out=STATE, handed_on=STATE))


def solution(mesh):
    cut = P(None, "lat", "lon")
    return jax.shard_map(
        body,
        mesh=mesh,
        in_specs=(cut, cut, cut, cut, cut, P("lat", "lon")),
        out_specs=(cut, cut, cut, cut),
        check_vma=False,
    )
```

```python
import jax
import jax.numpy as jnp
from jax import lax
from jax.experimental import pallas as pl
from jax.experimental.pallas import tpu as pltpu
from jax.sharding import PartitionSpec as P

TIME_STEP = 0.2
KAPPA = 0.1
VISCOSITY = 0.1
VERTICAL = 0.5
GRAVITY = 0.2
THERMAL = 0.3
HALINE = 0.2
CORIOLIS = 0.5

LEVELS = 15
ROWS = 96
COLS = 128
TILE = 8
BLOCKS = ROWS // TILE
PAD = TILE
TALL = ROWS + 2 * PAD
FIELDS = 5
STATE = 4
GROUPS = STATE + 3
SIGNS = (1.0, 1.0, -1.0, -1.0, 1.0)
PACK = 16 * 2 * FIELDS
WET_AT = 8 * LEVELS
EDGE_AT = WET_AT + 32
MESSAGE = EDGE_AT + 16
F32 = jnp.float32


def roll(x, shift, axis):
    return pltpu.roll(x, shift % x.shape[axis], axis)


def iota(shape, axis):
    return lax.broadcasted_iota(jnp.int32, shape, axis)


def links_of(wet):
    out = []
    above, ratio = None, None
    for k in range(LEVELS):
        below = VERTICAL * wet[k] * wet[k + 1] if k < LEVELS - 1 else None
        pivot = 1.0 + (below if below is not None else 0.0)
        if above is not None:
            pivot = pivot + above - above * ratio
        inverse = 1.0 / pivot
        ratio = below * inverse if below is not None else None
        out.append((above, inverse, ratio))
        above = below
    return out


def column_step(get, faces, links, spin, west=None, south=None, early=None):
    mix = KAPPA
    half = 0.5 * GRAVITY
    keep = (1.0 - 4.0 * TIME_STEP * VISCOSITY) / TIME_STEP
    done = [[], [], [], []]
    forward, loose = [], []
    east_sum = north_sum = None
    for k in range(LEVELS):
        w, oe, ow, on, os = faces(k)
        u, uE, uW, uN, uS = (get(2, k, 0, 0), get(2, k, 0, 1), get(2, k, 0, -1), get(2, k, 1, 0), get(2, k, -1, 0))
        v, vE, vW, vN, vS = (get(3, k, 0, 0), get(3, k, 0, 1), get(3, k, 0, -1), get(3, k, 1, 0), get(3, k, -1, 0))
        uNW, vSE = get(2, k, 1, -1), get(3, k, -1, 1)
        coef = []
        for speed, face in ((u, oe), (uW, ow), (v, on), (vS, os)):
            if face is None:
                coef.append(None)
                continue
            low = jnp.maximum(speed, 0.0) + mix
            coef.append((face * low, face * (low - speed)))
        tracers = []
        east, north = [], []
        for f in (0, 1):
            c, cE, cN = get(f, k, 0, 0), get(f, k, 0, 1), get(f, k, 1, 0)
            out_e = coef[0][0] * c - coef[0][1] * cE
            if west is None:
                out_e = out_e - (coef[1][0] * get(f, k, 0, -1) - coef[1][1] * c)
            out_n = coef[2][0] * c - coef[2][1] * cN
            out_s = south(f, k, out_n) if south else coef[3][0] * get(f, k, -1, 0) - coef[3][1] * c
            tracers.append((c - (out_n - out_s), out_e))
            east.append(cE - c)
            north.append(cN - c)
        loose.append(tracers)
        east_now = (half * HALINE) * east[1] - (half * THERMAL) * east[0]
        north_now = (half * HALINE) * north[1] - (half * THERMAL) * north[0]
        east_p = east_now if k == 0 else east_sum + east_now
        north_p = north_now if k == 0 else north_sum + north_now
        east_sum, north_sum = east_p + east_now, north_p + north_now
        done[2].append(oe * (keep * u + spin * ((v + vS) + (vE + vSE)) - east_p
                             + VISCOSITY * ((uE + uW) + (uN + uS))))
        done[3].append(on * (keep * v - spin * ((u + uN) + (uW + uNW)) - north_p
                             + VISCOSITY * ((vE + vW) + (vN + vS))))
    if early:
        early(done)
    for k in range(LEVELS):
        w = faces(k)[0]
        up, inverse, _ = links(k)
        now = []
        for f in (0, 1):
            kept, out = loose[k][f]
            x = w * (kept - (out - west(f, k, out) if west else out))
            now.append((x + up * forward[-1][f]) * inverse if k else x * inverse)
        forward.append(now)
    for f in (0, 1):
        value = forward[-1][f]
        back = [value]
        for k in range(LEVELS - 2, -1, -1):
            value = forward[k][f] + links(k)[2] * value
            back.append(value)
        done[f] = back[::-1]
    return done


def spin_of(row_index):
    angle = jnp.pi * ((row_index + 0.5) / (8.0 * ROWS) - 0.3)
    return (0.25 * CORIOLIS) * jnp.sin(angle)


SHIFTS = {0: (), 1: (), 2: (1, -1), 3: (-1, 1), 4: ()}


def eager(shift, fields):
    held = {}
    count = len(fields)
    for f in range(count):
        for k in range(LEVELS):
            held[f, k, 0, 0] = fields[f][k]
    for dj, di in ((0, 1), (0, -1), (1, 0), (-1, 0)):
        for f in range(count):
            for k in range(LEVELS):
                held[f, k, dj, di] = shift(fields[f][k], dj, di)
    for f in (2, 3):
        dj, di = SHIFTS[f]
        for k in range(LEVELS):
            held[f, k, dj, di] = shift(held[f, k, 0, di], dj, 0)
    return lambda f, k, dj, di: held[f, k, dj, di]


def faces_of(get):
    def faces(k):
        w = get(4, k, 0, 0)
        long = TIME_STEP * w
        return (w, long * get(4, k, 0, 1), long * get(4, k, 0, -1), long * get(4, k, 1, 0), long * get(4, k, -1, 0))

    return faces


def split3(x):
    a = x.astype(jnp.bfloat16)
    rest = x - a.astype(F32)
    b = rest.astype(jnp.bfloat16)
    return a, b, (rest - b.astype(F32)).astype(jnp.bfloat16)


def picked(terms, pick):
    return sum(jnp.dot(x, pick, preferred_element_type=F32) for x in terms)


def slide(slot, patterns):
    slot[...] = jnp.zeros(slot.shape, F32)
    p, lane = iota((TILE, COLS), 0), iota((TILE, COLS), 1)
    for i, moves in enumerate(patterns):
        hit = jnp.zeros((TILE, COLS), F32)
        for to, sources in moves.items():
            for source in sources:
                hit = jnp.where((lane == to) & (p == source), 1.0, hit)
        slot[120:128, COLS * i:COLS * i + COLS] = hit


def slid(slot, k):
    return slot[120 - 8 * k:248 - 8 * k, :].astype(jnp.bfloat16)


AROUND = {126: (0,), 127: (1,), 0: (2,), 1: (3,)}
NEXT1 = {127: (1,), 0: (6,)}
OWN1 = {0: (2,), 127: (5,)}
THIRD = {1: 0, 2: 3, 5: 4, 6: 7}


def with_third(moves):
    return {to: (p, THIRD[p]) for to, (p,) in moves.items()}


def pack_kernel(place, t, s, u, v, flag, tally, col_p, col_q, own_cols, rows, wet, t_in, s_in, u_in, v_in, open_e,
                link, spin, held_flag, held_tally, sems, gathered):
    field = (t_in, s_in, u_in, v_in)
    odd = place[1] % 2 == 1
    lane = iota((TILE, COLS), 1)
    sub = iota((TILE, COLS), 0)
    group = jnp.where(lane % 8 < 4, lane // 8, -1)
    inside = pl.ds(PAD, ROWS)
    half = ROWS // 2
    copies = [pltpu.make_async_copy(x, field[f].at[:, inside, :], sems.at[f]) for f, x in enumerate((t, s, u))]
    copies.append(pltpu.make_async_copy(v.at[:, 0:half, :], v_in.at[:, PAD:PAD + half, :], sems.at[3]))
    copies.append(pltpu.make_async_copy(flag, held_flag, sems.at[4]))
    copies.append(pltpu.make_async_copy(tally, held_tally, sems.at[5]))
    copies.append(pltpu.make_async_copy(v.at[:, half:ROWS, :], v_in.at[:, PAD + half:PAD + ROWS, :], sems.at[6]))
    for f in (4, 5, 0, 1, 2, 3, 6):
        copies[f].start()
    copies[4].wait()
    copies[5].wait()

    def gather(f, b):
        at = PAD + TILE * b
        out = jnp.zeros((TILE, COLS), F32)
        for k in range(LEVELS):
            x = (field[f] if f < STATE else wet)[k, at:at + TILE, :]
            out = jnp.where(group == k, roll(x, 8 * k + 2, 1), out)
        gathered[f, TILE * b:TILE * b + TILE, :] = out

    def couple(b):
        here = slice(TILE * b, TILE * b + TILE)
        column = [wet[k, PAD + TILE * b:PAD + TILE * b + TILE, :] for k in range(LEVELS)]
        for k, w in enumerate(column):
            open_e[k, here, :] = (TIME_STEP * w) * roll(w, COLS - 1, 1)
        for k, (up, inverse, ratio) in enumerate(links_of(column)):
            if up is not None:
                link[0, k, here, :] = up
            link[1, k, here, :] = inverse
            if ratio is not None:
                link[2, k, here, :] = ratio
        row = (place[0] * ROWS + b * TILE + iota((TILE, COLS), 0)).astype(F32)
        spin[here, :] = spin_of(row)

    for b in range(BLOCKS):
        here = slice(TILE * b, TILE * b + TILE)
        deep = held_tally[here, :]
        for k in range(LEVELS):
            wet[k, PAD + TILE * b:PAD + TILE * b + TILE, :] = jnp.where(k < deep, held_flag[k, here, :], 0).astype(F32)
    for f in (4, 0, 1, 2, 3):
        if f < STATE:
            copies[f].wait()
        for b in range(BLOCKS):
            if f == 3 and b == BLOCKS // 2:
                copies[6].wait()
            gather(f, b)
            if f != 3 and b % 4 == 3:
                couple(3 * (0 if f == 4 else f + 1) + b // 4)
        gathered[f, ROWS:COLS, :] = jnp.zeros((COLS - ROWS, COLS), F32)
    for f in range(FIELDS):
        own_cols[f] = gathered[f].T
    for side, first in ((0, PAD), (1, PAD + ROWS - 2)):
        for m in range(LEVELS + 4):
            parts = []
            for i in range(4):
                at = first - 2 * i
                if m < LEVELS:
                    parts.append(field[i][m, at:at + TILE, :])
                else:
                    k = min(4 * (m - LEVELS) + i, LEVELS - 1)
                    parts.append(wet[k, at:at + TILE, :])
            rows[side, TILE * m:TILE * m + TILE, :] = jnp.where(
                sub < 2, parts[0], jnp.where(sub < 4, parts[1], jnp.where(sub < 6, parts[2], parts[3])))
    for f in range(FIELDS):
        for c in range(2):
            last = own_cols[f, pl.ds(c, 16, stride=8), :]
            first = own_cols[f, pl.ds(2 + c, 16, stride=8), :]
            at = (2 * f + c) * 16
            col_p[at:at + 16, :] = jnp.where(odd, first, last)
            col_q[at:at + 16, :] = jnp.where(odd, last, first)


def spread_kernel(place, got_p, got_q, own_cols, rows, _, strip, ghost, own, to_x, to_y, turned):
    odd = place[1] % 2 == 1
    lat_odd = place[0] % 2 == 1
    fold = place[0] == 7
    for f in range(FIELDS):
        for c in range(2):
            at = (2 * f + c) * 16
            a, b = got_p[at:at + 16, :], got_q[at:at + 16, :]
            west, east = jnp.where(odd, a, b), jnp.where(odd, b, a)
            strip[f, pl.ds(c, 16, stride=8), :] = west
            strip[f, pl.ds(6 + c, 16, stride=8), :] = east
            strip[f, pl.ds(2 + c, 16, stride=8), :] = own_cols[f, pl.ds(2 + c, 16, stride=8), :]
            strip[f, pl.ds(4 + c, 16, stride=8), :] = own_cols[f, pl.ds(c, 16, stride=8), :]
            turned[f, pl.ds(c, 16, stride=8), :] = west
            turned[f, pl.ds(2 + c, 16, stride=8), :] = east
            turned[f, pl.ds(4 + c, 16, stride=8), :] = west
            turned[f, pl.ds(6 + c, 16, stride=8), :] = east
    for f in range(FIELDS):
        ghost[f] = turned[f].T
    for f in range(FIELDS):
        own[0, EDGE_AT + 2 * f:EDGE_AT + 2 * f + 2, :] = ghost[f, 0:2, :]
        own[1, EDGE_AT + 2 * f:EDGE_AT + 2 * f + 2, :] = ghost[f, ROWS - 2:ROWS, :]
    for side in range(2):
        own[side, 0:EDGE_AT, :] = rows[side]
        own[side, EDGE_AT + 2 * FIELDS:MESSAGE, :] = jnp.zeros((MESSAGE - EDGE_AT - 2 * FIELDS, COLS), F32)
    low, high = own[0], own[1]
    to_x[...] = jnp.where(lat_odd, high, low)
    to_y[...] = jnp.where(lat_odd, low, high)

    @pl.when(fold)
    def _():
        a, b = iota((COLS, COLS), 0), iota((COLS, COLS), 1)
        mirror = (a + b == COLS - 1).astype(jnp.bfloat16)
        mirror_edge = ((a // 8 == b // 8) & (a % 8 < 4) & (a % 8 + b % 8 == 3)).astype(jnp.bfloat16)
        to_x[0:EDGE_AT, :] = picked(split3(own[1, 0:EDGE_AT, :]), mirror)
        to_x[EDGE_AT:MESSAGE, :] = picked(split3(own[1, EDGE_AT:MESSAGE, :]), mirror_edge)


def first_kernel(t, s, u, v, wet, open_e, link, spin, field1, flux):
    field = (t, s, u, v)

    def step_block(b):
        r = PAD + TILE * b
        src = slice(TILE * b, TILE * b + TILE)

        def get(f, k, dj, di):
            x = field[f][k, r + dj:r + dj + TILE, :]
            return roll(x, -di, 1) if di else x

        def faces(k):
            w = wet[k, r:r + TILE, :]
            return (w, open_e[k, src, :], None, (TIME_STEP * w) * wet[k, r + 1:r + 1 + TILE, :], None)

        def south(f, k, x):
            flux[f, k, r:r + TILE, :] = x
            return flux[f, k, r - 1:r - 1 + TILE, :]

        moved = column_step(get, faces, lambda k: tuple(link[i, k, src, :] for i in range(3)), spin[src, :],
                            lambda f, k, x: roll(x, 1, 1), south)
        for f in range(STATE):
            for k in range(LEVELS):
                field1[f, k, r:r + TILE, :] = moved[f][k]

    for b in range(BLOCKS):
        step_block(b)


def second_kernel(place, field1, wet, open_e, link, spin, strip, ghost, t, s, u, v, inner, inner_ghost, blocks,
                  state, outs, ghost1, turned, beside, face, flux, slot, slot_third, terms, sems):
    first_row = place[0] * ROWS
    lane = iota((TILE, COLS), 1)
    sub = iota((TILE, COLS), 0)

    def strip_shift(x, dj, di):
        if di:
            x = roll(x, -di, 0)
        return roll(x, -dj, 1) if dj else x

    values = [[strip[f, 8 * k:8 * k + 8, :] for k in range(LEVELS)] for f in range(FIELDS)]
    get1 = eager(strip_shift, values)
    row = (first_row + iota((1, COLS), 1)).astype(F32)
    links1 = links_of(values[4])
    moved = column_step(get1, faces_of(get1), lambda k: links1[k], spin_of(row))
    for f in range(STATE):
        for k in range(LEVELS):
            turned[f, 8 * k:8 * k + 8, :] = moved[f][k]
    faces1 = faces_of(get1)
    for f in range(2):
        for k in range(LEVELS):
            c, speed, face_e = moved[f][k], moved[2][k], faces1(k)[1]
            low = jnp.maximum(speed, 0.0) + KAPPA
            turned[STATE + f, 8 * k:8 * k + 8, :] = roll(face_e * (low * c - (low - speed) * roll(c, -1, 0)), 5, 0)
    for k in range(LEVELS):
        w = values[4][k]
        turned[GROUPS - 1, 8 * k:8 * k + 8, :] = jnp.where(sub == 2, roll(w, 1, 0), roll(w, -1, 0))
    for g in range(GROUPS):
        turned[g, 8 * LEVELS:COLS, :] = jnp.zeros((COLS - 8 * LEVELS, COLS), F32)
    for g in range(GROUPS):
        ghost1[g] = turned[g].T

    inside = pl.ds(PAD, ROWS)
    wide = iota((ROWS, COLS), 1)
    edge_lane = (wide == 0) | (wide == COLS - 1)
    place_in = wide % 8
    second = (place_in == 1) | (place_in == 2) | (place_in == 5) | (place_in == 6)
    from_east = (place_in == 0) | (place_in == 4)
    slide(slot, (NEXT1, OWN1))
    slide(slot_third, (with_third(NEXT1), with_third(OWN1)))
    for g in range(GROUPS):
        x = ghost1[g, 0:ROWS, :]
        a = x.astype(jnp.bfloat16)
        rest = x - a.astype(F32)
        b = rest.astype(jnp.bfloat16).astype(F32)
        c = rest - b
        terms[ROWS * g:ROWS * g + ROWS, 0:COLS] = a
        terms[ROWS * g:ROWS * g + ROWS, COLS:2 * COLS] = jnp.where(
            second, b, jnp.where(from_east, roll(c, -1, 1), roll(c, 1, 1))).astype(jnp.bfloat16)
    for k in range(LEVELS):
        pick = jnp.concatenate([slid(slot, k), slid(slot_third, k)], axis=0)
        found = jnp.dot(terms[...], pick, preferred_element_type=F32)
        face[k] = found[ROWS * (GROUPS - 1):, COLS:]
        for f in range(STATE + 2):
            beside[f, k, inside, :] = found[ROWS * f:ROWS * f + ROWS, :COLS]
        for f in range(STATE):
            state[f, k, inside, :] = jnp.where(edge_lane, found[ROWS * f:ROWS * f + ROWS, COLS:], field1[f, k, inside, :])

    def copies(b):
        src = slice(TILE * b, TILE * b + TILE)
        return [pltpu.make_async_copy(outs.at[f, :, src, :], x.at[:, src, :], sems.at[f, b])
                for f, x in enumerate((t, s, u, v))]

    def step_block(b):
        r = PAD + TILE * b
        src = slice(TILE * b, TILE * b + TILE)

        def get(f, k, dj, di):
            here = slice(r + dj, r + dj + TILE)
            x = state[f, k, here, :]
            if di == 0:
                return x
            return roll(jnp.where(lane == (0 if di > 0 else COLS - 1), beside[f, k, here, :], x), -di, 1)

        def faces(k):
            w = wet[k, r:r + TILE, :]
            long = TIME_STEP * w
            return (w, jnp.where(lane == COLS - 1, long * face[k, src, :], open_e[k, src, :]), None,
                    long * wet[k, r + 1:r + 1 + TILE, :], None)

        def west(f, k, x):
            return jnp.where(lane == 0, beside[STATE + f, k, r:r + TILE, :], roll(x, 1, 1))

        def south(f, k, x):
            flux[f, k, r:r + TILE, :] = x
            return flux[f, k, r - 1:r - 1 + TILE, :]

        moved = column_step(get, faces, lambda k: tuple(link[i, k, src, :] for i in range(3)), spin[src, :], west, south)
        for f in range(STATE):
            for k in range(LEVELS):
                if 0 < b < BLOCKS - 1:
                    outs[f, k, src, :] = moved[f][k]
                else:
                    blocks[b // (BLOCKS - 1), f, k] = moved[f][k]
        if 0 < b < BLOCKS - 1:
            for c in copies(b):
                c.start()

    for b in range(BLOCKS):
        step_block(b)

    for f in range(FIELDS):
        for k in range(LEVELS):
            src = state.at[f, k] if f < STATE else wet.at[k]
            inner[f, k] = jnp.where(sub < 4, src[PAD - 1:PAD + 7, :], src[PAD + 89:PAD + 97, :])
        edge = ghost1.at[f] if f < STATE else ghost.at[4]
        inner_ghost[f] = jnp.where(sub < 4, roll(edge[0:8, :], 1, 0), edge[89:97, :])
    for b in range(1, BLOCKS - 1):
        for c in copies(b):
            c.wait()


def edge_kernel(place, own, got_x, got_y, inner, inner_ghost, blocks, t, s, u, v, t_out, s_out, u_out, v_out,
                low, high, mine_low, mine_high, slot, ring, lead, moved1, ring2, lead2, final, sems):
    lat = place[0]
    odd = lat % 2 == 1
    fold = lat == 7
    sub = iota((TILE, COLS), 0)
    lane = iota((TILE, COLS), 1)
    tile = slice(PAD, PAD + TILE)
    body_rows = slice(PAD, PAD + MESSAGE)
    from_x, from_y = got_x[...], got_y[...]
    low[body_rows, :] = jnp.where(odd, from_y, jnp.where(lat == 0, 0.0, from_x))
    high[body_rows, :] = jnp.where(odd, from_x, from_y)
    mine_low[body_rows, :] = own[0]
    mine_high[body_rows, :] = own[1]
    slide(slot, (AROUND, NEXT1))

    def rows(ref, at, early):
        return ref[PAD + at - early:PAD + at - early + TILE, :]

    def where_of(f, k):
        return 8 * k + 2 * f if f < STATE else WET_AT + 2 * k

    def stack(at, sign):
        top = jnp.where(fold, sign * rows(high, at, 5), rows(high, at, 6))
        return jnp.where(sub < 2, rows(low, at, 0), jnp.where(
            sub < 4, rows(mine_low, at, 2), jnp.where(sub < 6, rows(mine_high, at, 4), top)))

    def stack_fold(at, sign):
        return jnp.where(sub < 2, rows(high, at, 0), sign * rows(mine_high, at, 1))

    def spreads(tiles):
        terms = split3(jnp.concatenate(tiles, axis=0))
        out = []
        for k in range(LEVELS):
            found = picked(terms, slid(slot, k))
            out.append([(found[TILE * i:TILE * i + TILE, :COLS], found[TILE * i:TILE * i + TILE, COLS:])
                        for i in range(len(tiles))])
        return out

    def ring_getter(build, edges, back):
        held = {}
        for f in range(FIELDS):
            for k in range(LEVELS):
                x, g = build(where_of(f, k), SIGNS[f]), edges[k][f][0]
                ring[f, k, tile, :COLS] = x
                ring[f, k, tile, COLS:] = g
                held[f, k, 0, 0] = (x, g)
        for f in range(FIELDS):
            for k in range(LEVELS):
                x, g = held[f, k, 0, 0]
                a, b = jnp.where(lane == 0, g, x), jnp.where(lane == 0, x, g)
                held[f, k, 0, back] = (roll(a, -1, 1), roll(b, -1, 1))
                a, b = jnp.where(lane == COLS - 1, g, x), jnp.where(lane == COLS - 1, x, g)
                held[f, k, 0, -back] = (roll(a, 1, 1), roll(b, 1, 1))
        for f, di in ((2, -1), (3, 1)):
            for k in range(LEVELS):
                x, g = held[f, k, 0, di]
                lead[f - 2, k, tile, :COLS] = x
                lead[f - 2, k, tile, COLS:] = g

        def get(f, k, dj, di):
            if dj == 0:
                return jnp.concatenate(held[f, k, 0, di], axis=1)
            ref = lead.at[f - 2, k] if di else ring.at[f, k]
            return ref[PAD + dj:PAD + dj + TILE, :]

        return get

    def one_step(get, row, early=None):
        links = links_of([get(4, k, 0, 0) for k in range(LEVELS)])
        return column_step(get, faces_of(get), lambda k: links[k], spin_of(row), early=early)

    def global_rows(low_row, high_row):
        i = iota((TILE, 1), 0)
        return (lat * ROWS + i + jnp.where(i < 4, low_row, high_row - 4)).astype(F32)

    near_tiles = [inner_ghost[f] for f in range(FIELDS)]
    placed = spreads([stack(EDGE_AT + 2 * f, SIGNS[f]) for f in range(FIELDS)] + near_tiles)
    first = one_step(ring_getter(stack, placed, 1), global_rows(-2, ROWS - 2))
    for f in range(STATE):
        for k in range(LEVELS):
            moved1[f, k, tile, :] = first[f][k]
    for k in range(LEVELS):
        moved1[STATE, k, tile, :] = ring[STATE, k, tile, :]

    @pl.when(fold)
    def _():
        edges = spreads([stack_fold(EDGE_AT + 2 * f, SIGNS[f]) for f in range(FIELDS)])
        row = jnp.full((TILE, 1), 8.0 * ROWS - 1.0, F32)
        mirror = one_step(ring_getter(stack_fold, edges, -1), row)
        wide = iota((TILE, 2 * COLS), 0)
        for f in range(STATE):
            for k in range(LEVELS):
                ring[f, k, tile, :] = mirror[f][k]
        for f in range(STATE):
            for k in range(LEVELS):
                moved1[f, k, tile, :] = jnp.where(
                    wide == 6, SIGNS[f] * ring[f, k, PAD - 5:PAD + 3, :], moved1[f, k, tile, :])

    held = {}
    ghosts = {}
    for f in range(FIELDS):
        for k in range(LEVELS):
            down, up = moved1[f, k, PAD + 1:PAD + 1 + TILE, :], moved1[f, k, PAD - 1:PAD - 1 + TILE, :]
            near = placed[k][FIELDS + f][1 if f < STATE else 0]
            both = [jnp.where(sub < 2, down[:, c], jnp.where(sub < 6, mid, up[:, c]))
                    for c, mid in ((slice(0, COLS), inner[f, k]), (slice(COLS, 2 * COLS), near))]
            held[f, k, 0, 0], ghosts[f, k] = both
            ring2[f, k, tile, :] = both[0]
    for f in range(FIELDS):
        for k in range(LEVELS):
            x, g = held[f, k, 0, 0], ghosts[f, k]
            held[f, k, 0, 1] = roll(jnp.where(lane == 0, g, x), -1, 1)
            held[f, k, 0, -1] = roll(jnp.where(lane == COLS - 1, g, x), 1, 1)
    for f, di in ((2, -1), (3, 1)):
        for k in range(LEVELS):
            lead2[f - 2, k, tile, :] = held[f, k, 0, di]

    def get2(f, k, dj, di):
        if dj == 0:
            return held[f, k, 0, di]
        ref = lead2.at[f - 2, k] if di else ring2.at[f, k]
        return ref[PAD + dj:PAD + dj + TILE, :]

    def finish(f, levels):
        for k in range(LEVELS):
            ring2[f, k, tile, :] = levels[k]
        for k in range(LEVELS):
            final[0, f, k] = jnp.where(sub < 2, ring2[f, k, PAD + 1:PAD + 1 + TILE, :], blocks[0, f, k])
            final[1, f, k] = jnp.where(sub >= 6, ring2[f, k, PAD - 1:PAD - 1 + TILE, :], blocks[1, f, k])
        x = (t_out, s_out, u_out, v_out)[f]
        copies = [pltpu.make_async_copy(final.at[side, f], x.at[:, first_row:first_row + TILE, :], sems.at[side, f])
                  for side, first_row in ((0, 0), (1, ROWS - TILE))]
        for c in copies:
            c.start()
        return copies

    flying = []

    def early(done):
        for f in (2, 3):
            flying.extend(finish(f, done[f]))

    last = one_step(get2, global_rows(-1, ROWS - 3), early)
    for f in (0, 1):
        flying.extend(finish(f, last[f]))
    for c in flying:
        c.wait()


def limit(mebibytes):
    return pltpu.CompilerParams(vmem_limit_bytes=mebibytes * 1024 * 1024)


def call(kernel, place, args, outs, scratch, mebibytes, flops, far_in=0, far_out=0, handed_on=0):
    far = [i < far_in or i >= len(args) - handed_on for i in range(len(args))]
    vmem, hbm = pl.BlockSpec(memory_space=pltpu.VMEM), pl.BlockSpec(memory_space=pltpu.HBM)
    args = [pltpu.with_memory_space_constraint(a, pltpu.HBM if there else pltpu.VMEM) for a, there in zip(args, far)]
    return pl.pallas_call(
        kernel,
        out_shape=[jax.ShapeDtypeStruct(o, F32) if i < far_out else pltpu.VMEM(o, F32) for i, o in enumerate(outs)],
        in_specs=[pl.BlockSpec(memory_space=pltpu.SMEM)] + [hbm if there else vmem for there in far],
        out_specs=[hbm if i < far_out else vmem for i in range(len(outs))],
        scratch_shapes=[pltpu.VMEM(x, F32) if isinstance(x, tuple) else x for x in scratch],
        input_output_aliases={1 + len(args) - handed_on + i: i for i in range(handed_on)},
        compiler_params=limit(mebibytes),
        cost_estimate=pl.CostEstimate(flops=flops, bytes_accessed=4_000_000, transcendentals=0),
    )(place, *args)


def device(lon, lat, lats, lons):
    return lon % lons * lats + lat


def body(t, s, u, v, flag, tally):
    lons, lats = lax.axis_size("lon"), lax.axis_size("lat")
    lat, lon = lax.axis_index("lat"), lax.axis_index("lon")
    place = jnp.stack([lat, lon]).astype(jnp.int32)
    pairs_p, pairs_q, pairs_x, pairs_y = [], [], [], []
    for a in range(lats):
        for o in range(lons):
            here = device(o, a, lats, lons)
            pairs_p.append((here, device(o ^ 1, a, lats, lons)))
            pairs_q.append((here, device(o + 1 if o % 2 else o - 1, a, lats, lons)))
            pairs_y.append((here, device(o, a ^ 1, lats, lons)))
            next_lat = a + 1 if a % 2 else a - 1
            inside = 0 <= next_lat < lats
            pairs_x.append((here, device(o, next_lat, lats, lons) if inside else device(lons - 1 - o, a, lats, lons)))

    def send(x, pairs):
        return lax.ppermute(x, ("lon", "lat"), pairs)

    edges = (2, STATE, LEVELS, TILE, COLS)
    deep, tall, square = (LEVELS, ROWS, COLS), (LEVELS, TALL, COLS), (FIELDS, COLS, COLS)
    message = (MESSAGE, COLS)
    col_p, col_q, own_cols, rows, wet, *padded, open_e, link, spin = call(
        pack_kernel, place, (t, s, u, v, flag, tally), [(PACK, COLS), (PACK, COLS), square, (2, EDGE_AT, COLS)] + [tall] * 5
        + [deep, (3,) + deep, (ROWS, COLS)], [pltpu.VMEM(deep, jnp.int32), pltpu.VMEM((ROWS, COLS), jnp.int32), pltpu.SemaphoreType.DMA((7,)), square],
        12, 1_000_000, far_in=6)
    got_p, got_q = send(col_p, pairs_p), send(col_q, pairs_q)
    field1, = call(lambda _, *refs: first_kernel(*refs), place, (*padded, wet, open_e, link, spin), [(STATE,) + tall],
                   [(2,) + tall], 12, 40_000_000)
    strip, ghost, own, to_x, to_y = call(
        spread_kernel, place, (got_p, got_q, own_cols, rows, field1), [square, square, (2, MESSAGE, COLS), message, message],
        [square], 4, 1_000_000)
    got_x, got_y = send(to_x, pairs_x), send(to_y, pairs_y)
    *fields, inner, inner_ghost, blocks = call(
        second_kernel, place, (field1, wet, open_e, link, spin, strip, ghost),
        [deep] * STATE + [(FIELDS, LEVELS, TILE, COLS), (FIELDS, TILE, COLS), edges],
        [(STATE,) + tall, (STATE,) + deep, (GROUPS, COLS, COLS), (GROUPS, COLS, COLS), (STATE + 2,) + tall, deep,
         (2,) + tall, (248, 2 * COLS), (248, 2 * COLS), pltpu.VMEM((GROUPS * ROWS, 2 * COLS), jnp.bfloat16),
         pltpu.SemaphoreType.DMA((STATE, BLOCKS))], 20, 50_000_000, far_out=STATE)
    near, wide = (FIELDS, LEVELS, 3 * TILE, COLS), (FIELDS, LEVELS, 3 * TILE, 2 * COLS)
    padded = (MESSAGE + 2 * PAD, COLS)
    return tuple(call(
        edge_kernel, place, (own, got_x, got_y, inner, inner_ghost, blocks, *fields), [deep] * STATE,
        [padded] * 4 + [(248, 2 * COLS), wide, (2,) + wide[1:], wide, near, (2,) + near[1:], edges,
                        pltpu.SemaphoreType.DMA((2, STATE))], 16, 2_000_000, far_out=STATE, handed_on=STATE))


def solution(mesh):
    cut = P(None, "lat", "lon")
    return jax.shard_map(
        body,
        mesh=mesh,
        in_specs=(cut, cut, cut, cut, cut, P("lat", "lon")),
        out_specs=(cut, cut, cut, cut),
        check_vma=False,
    )
```
